256 devices in a mesh: rep: 2 (over x_lo), tok: 2 (over x_hi), voc: 64 (over y, z, core).
Axes of the slice: x: 4 (x_hi: 2, x_lo: 2; x = x_hi * 2 + x_lo), y: 4, z: 8, core: 2. Of those that a mesh axis runs over, the one named last changes fastest.
Arguments:
- hidden: bfloat16 [2, 768, 3584], P('rep', 'tok'), may hold values from -30 to 30
- head: bfloat16 [3584, 131072], P('tok', 'voc'), may hold values from -0.3125 to 0.3125
- targets: int32 [768], P('tok'), may hold values from 0 to 131071
- loss_mask: int32 [768], P('tok'), may hold values 0 or 1
Outputs:
- grad_hidden: bfloat16 [2, 768, 3584], P('rep', ('tok', 'voc'))
- token_loss: float32 [2, 768], P('rep', 'tok')
The draws below stay inside these ranges and needn't reach their ends.
All inputs are finite; a program needn't handle non-finite values. No bound on the sum of `loss_mask` on one device may be relied on, other than what follows from the above.
Results may differ from the reference program's by a relative error of at most 0.0065.
Values may be sent and summed in bfloat16 or wider, within the bound.
No kernel may reach another device: no remote copies, remote signals or barrier semaphores. Data moves between devices by JAX's collectives and lax.ppermute only.
A program may use at most 128 MiB of HBM per device.

```python
import math
import jax
import jax.numpy as jnp
import numpy as np
from jax import lax

D = 3584
TOK_DEV = 384
VOCAB = 131072
TOKENS = 768
N_TOK = 2


def draw_hidden(key, part):
    key = jax.random.fold_in(key, 11)
    first_key, second_key = jax.random.split(key, 2)
    base = jnp.clip(jax.random.normal(first_key, (2, TOKENS, D), jnp.float32), -4.0, 4.0)
    mixed = jnp.stack([base[0], 0.8 * base[0] + 0.6 * base[1]])
    row_scale = jnp.exp(jax.random.uniform(second_key, (1, TOKENS, 1), jnp.float32, math.log(0.5), math.log(5.0)))
    return (mixed * row_scale).astype(jnp.bfloat16)


def place_ends(entries, rng, smallest, top_value):
    index_at = [jax.random.randint(jax.random.fold_in(rng, axis), (), 0, length) for axis, length in enumerate(entries.shape)]
    main_axis = entries.shape.index(max(entries.shape))
    beside = index_at[:main_axis] + [(index_at[main_axis] + 1) % entries.shape[main_axis]] + index_at[main_axis + 1:]
    return entries.at[tuple(index_at)].set(smallest).at[tuple(beside)].set(top_value)


def steps_of(own_key, shape, shards, smallest, top_value):
    def one(axis_at, shards_of):
        steps = jax.random.uniform(jax.random.fold_in(jax.random.fold_in(own_key, 6), axis_at), (shards_of,), jnp.float32, smallest / len(shards), top_value / len(shards))
        return jnp.repeat(jnp.exp(steps), shape[axis_at] // shards_of).reshape((-1,) + (1,) * (len(shape) - axis_at - 1))

    loudness = one(*shards[0])
    for cut in shards[1:]:
        loudness = loudness * one(*cut)
    return loudness


def wide_ids(rng, dims, number_of, skew):
    weights = [min(1 << octave, number_of + 1 - (1 << octave)) * (1 << 20) // math.isqrt((1 << octave) ** skew) + 1 for octave in range((number_of + 1).bit_length()) if 1 << octave <= number_of]
    scale = 1 + sum(weights) // (1 << 30)
    table = np.cumsum(np.array([max(1, weight // scale) for weight in weights]))
    lot = jax.random.randint(jax.random.fold_in(rng, 1), dims, 0, int(table[len(weights) - 1]))
    start = jnp.left_shift(1, jnp.searchsorted(jnp.asarray(table, jnp.int32), lot, side="right").astype(jnp.int32))
    grade = start - 1 + jax.random.randint(jax.random.fold_in(rng, 4), dims, 0, 1 << 30) % jnp.minimum(start, number_of + 1 - start)
    return jax.random.permutation(jax.random.fold_in(rng, 2), number_of)[grade].astype(jnp.int32)


def normal_values(rng, dims, deviation, bound, shards=(), kind=jnp.bfloat16):
    array = jax.random.normal(rng, dims, jnp.float32) * deviation
    if len(shards) > 0:
        array = steps_of(rng, dims, shards, -0.22, 0.18) * array
    return jnp.clip(array, min=-bound, max=bound).astype(kind)


def setup_inputs(seed: int = 0) -> dict:
    key_list = jax.random.split(jax.random.key(seed), 5)
    return {
        "hidden": draw_hidden(jax.random.fold_in(key_list[4], 71), 0),
        "head": normal_values(key_list[1], (D, VOCAB), (D // 9) ** -0.5, 0.3125, ((0, 2), (1, 64))),
        "targets": place_ends(wide_ids(key_list[2], (TOKENS,), VOCAB, 2), jax.random.fold_in(key_list[2], 3), 0, VOCAB - 1).astype(jnp.int32),
        "loss_mask": place_ends((jax.random.randint(key_list[3], (TOKENS,), 0, 4) < 3).astype(jnp.int32), jax.random.fold_in(key_list[3], 1), 0, 1),
    }


softcap_limit = 30.0
kl_weight = 0.5
loss_scale = 16.0


def capped(raw_logits):
    return softcap_limit * jnp.tanh(raw_logits / softcap_limit)


def token_block(hidden, head, targets, loss_mask):
    logits_list = [capped(jnp.dot(hidden[replica], head, preferred_element_type=jnp.float32)) for replica in range(2)]
    shared = [lax.optimization_barrier(values.astype(jnp.bfloat16)).astype(jnp.float32) for values in logits_list]
    columns = lax.broadcasted_iota(jnp.int32, (1, head.shape[1]), 1)
    target_hit = columns == targets[:, None]
    weights_tok = loss_mask.astype(jnp.float32)
    grads = []
    losses = []
    for replica in range(2):
        own_logits = logits_list[replica]
        partner_logits = shared[1 - replica]
        own_exp = jnp.exp(own_logits)
        own_total = jnp.sum(own_exp, axis=1)
        picked = jnp.sum(jnp.where(target_hit, own_logits, jnp.float32(0.0)), axis=1)
        partner_exp = jnp.exp(partner_logits)
        partner_total = jnp.sum(partner_exp, axis=1)
        cross = jnp.sum(partner_exp * (partner_logits - own_logits), axis=1)
        own_lse = jnp.log(own_total)
        partner_lse = jnp.log(partner_total)
        losses.append(weights_tok * (own_lse - picked + kl_weight * (cross / partner_total - partner_lse + own_lse)))
        logit_grad = (loss_scale * weights_tok)[:, None] * (
            (1.0 + kl_weight) * own_exp / own_total[:, None]
            - target_hit.astype(jnp.float32)
            - kl_weight * partner_exp / partner_total[:, None]) * (1.0 - (own_logits / softcap_limit) ** 2)
        grad_low = logit_grad.astype(jnp.bfloat16)
        grads.append(lax.dot_general(grad_low, head, (((1,), (1,)), ((), ())),
                                     preferred_element_type=jnp.float32).astype(jnp.bfloat16))
    return jnp.stack(grads), jnp.stack(losses)


def reference(hidden, head, targets, loss_mask):
    def one_block(index):
        begin = (index * TOK_DEV).astype(jnp.int32)
        return token_block(lax.dynamic_slice_in_dim(hidden, begin, TOK_DEV, 1), head,
                           lax.dynamic_slice_in_dim(targets, begin, TOK_DEV, 0),
                           lax.dynamic_slice_in_dim(loss_mask, begin, TOK_DEV, 0))

    grads, losses = lax.map(one_block, jnp.arange(N_TOK, dtype=jnp.int32))
    grad_hidden = jnp.transpose(grads, (1, 0, 2, 3)).reshape(2, N_TOK * TOK_DEV, D)
    token_loss = jnp.transpose(losses, (1, 0, 2)).reshape(2, N_TOK * TOK_DEV)
    return grad_hidden, token_loss
```

```python
import jax
import jax.numpy as jnp
from jax import lax
from jax.sharding import PartitionSpec as P

softcap_limit = 30.0
kl_weight = 0.5
loss_scale = 16.0

N_Y, N_Z, N_C, N_X = 4, 8, 2, 4
LINE = ("rep", "tok")


def line_xor(block, k):
    k = (k % 2) * 2 + k // 2
    return lax.ppermute(block, LINE, [(x, x ^ k) for x in range(N_X)])


def voc_xor(block, k):
    return lax.ppermute(block, "voc", [(v, v ^ k) for v in range(N_Y * N_Z * N_C)])


def tree_sum(values):
    values = list(values)
    while len(values) > 1:
        values = [a + b for a, b in zip(values[::2], values[1::2])]
    return values[0]


def sum_over(stats):
    stats = tree_sum([stats] + [line_xor(stats, k) for k in (1, 2, 3)])
    stats = tree_sum([stats, voc_xor(stats, 1)])
    stats = tree_sum([stats] + [voc_xor(stats, 16 * k) for k in (1, 2, 3)])
    stats = tree_sum([stats] + [voc_xor(stats, 2 * k) for k in range(1, 8)])
    return stats


def capped(raw_logits):
    return softcap_limit * jnp.tanh(raw_logits / softcap_limit)


def gather_hidden(states, voc):
    k = voc % 16
    c, y, zh = k // 8, (k // 2) % 4, k % 2
    d_block = voc // 16
    slab = lax.dynamic_slice(states, (y * 96 + zh * 48, d_block * 896), (48, 896))
    x = lax.axis_index("tok") * 2 + lax.axis_index("rep")
    slabs = jnp.stack([slab] + [line_xor(slab, j) for j in (1, 2, 3)])
    out = lax.broadcasted_iota(jnp.int32, (96, 192), 0)
    src = lax.broadcasted_iota(jnp.int32, (96, 192), 1)
    rep, z, tok, i = out // 48, out % 48 // 12, out % 12 // 6, out % 6
    wanted = ((tok * 2 + rep) ^ x) * 48 + z * 12 + c * 6 + i
    pick = (src == wanted).astype(jnp.bfloat16)
    piece = jnp.dot(pick, slabs.reshape(192, 896), preferred_element_type=jnp.float32)
    piece = piece.astype(jnp.bfloat16).reshape(1, 2, 48, 896)
    full = lax.all_gather(piece, "voc", axis=0, tiled=True)
    return full.reshape(4, 16, 2, 48, 896)


def shards(hidden, head, targets, loss_mask):
    rep, tok, voc = (lax.axis_index(a) for a in ("rep", "tok", "voc"))
    x = tok * 2 + rep
    width = head.shape[1] // N_X

    def quarter(q):
        return lax.dynamic_slice(head, (0, q * width), (head.shape[0], width))

    other_half = line_xor(quarter(3 - x), 3)
    own_half = quarter(x)
    rows = gather_hidden(hidden[0], voc)
    rows = rows.transpose(2, 1, 3, 0, 4).reshape(2 * 768, 3584)

    low = jnp.where(tok == 0, own_half, other_half)
    high = jnp.where(tok == 0, other_half, own_half)
    raw = jnp.dot(rows[:, :1792], low, preferred_element_type=jnp.float32) + jnp.dot(
        rows[:, 1792:], high, preferred_element_type=jnp.float32
    )
    logits = capped(raw).reshape(2, 768, width)
    shared = lax.optimization_barrier(logits.astype(jnp.bfloat16)).astype(jnp.float32)
    partner = shared[::-1]

    scal = jnp.stack([targets, loss_mask])
    both = jnp.stack([scal, line_xor(scal, 2)])
    both = jnp.where(tok == 0, both, both[::-1])
    both = both.reshape(2, 2, 4, 8, 2, 6).transpose(1, 4, 2, 3, 0, 5).reshape(2, 768)
    row_targets, row_mask = both[0], both[1].astype(jnp.float32)

    columns = voc * head.shape[1] + x * width + lax.broadcasted_iota(jnp.int32, (1, 1, width), 2)
    hit = columns == row_targets[None, :, None]
    own_exp = jnp.exp(logits)
    partner_exp = jnp.exp(partner)
    stats = jnp.stack([
        jnp.sum(own_exp, axis=2),
        jnp.sum(partner_exp, axis=2),
        jnp.sum(jnp.where(hit, logits, 0.0), axis=2),
        jnp.sum(partner_exp * (partner - logits), axis=2),
    ])
    own_total, partner_total, picked, cross = sum_over(stats)

    own_lse, partner_lse = jnp.log(own_total), jnp.log(partner_total)
    losses = row_mask * (
        own_lse - picked + kl_weight * (cross / partner_total - partner_lse + own_lse)
    )
    loss = lax.dynamic_index_in_dim(losses, rep, 0, keepdims=False)
    loss = loss.reshape(2, 4, 8, 2, 6)
    loss = lax.dynamic_index_in_dim(loss, tok, 3, keepdims=False)
    token_loss = loss.transpose(1, 2, 0, 3).reshape(1, 384)

    grad = (loss_scale * row_mask)[None, :, None] * (
        (1.0 + kl_weight) * own_exp / own_total[..., None]
        - hit.astype(jnp.float32)
        - kl_weight * partner_exp / partner_total[..., None]
    ) * (1.0 - (logits / softcap_limit) ** 2)
    grad = grad.astype(jnp.bfloat16)

    mine = lax.dynamic_index_in_dim(grad, rep, 0, keepdims=False)
    theirs = lax.dynamic_index_in_dim(grad, 1 - rep, 0, keepdims=False)
    parts = [mine, line_xor(theirs, 1), line_xor(mine, 2), line_xor(theirs, 3)]
    terms = sum(
        lax.dot_general(p, quarter(x ^ j), (((1,), (1,)), ((), ())), preferred_element_type=jnp.float32)
        for j, p in enumerate(parts)
    )

    def scatter(parts, me, xor, count):
        low = parts.astype(jnp.bfloat16)
        total = lax.dynamic_index_in_dim(parts, me, 0, keepdims=False)
        got = [
            voc_xor(lax.dynamic_index_in_dim(low, me ^ k, 0, keepdims=False), k * xor)
            for k in range(1, count)
        ]
        for g in got:
            total = total + g.astype(jnp.float32)
        return total

    c, y, z = voc % 2, voc // 16, (voc // 2) % 8
    part = scatter(terms.reshape(2, 384, 1792), c, 1, 2)
    part = scatter(part.reshape(4, 96, 1792), y, 16, 4)
    part = scatter(part.reshape(8, 12, 1792), z, 2, 8)
    part = part.astype(jnp.bfloat16).reshape(2, 6, 1792)
    keep = lax.dynamic_index_in_dim(part, tok, 0, keepdims=False)
    sent = lax.dynamic_index_in_dim(part, 1 - tok, 0, keepdims=False)
    got = line_xor(sent, 2)
    out = jnp.where(
        tok == 0, jnp.concatenate([keep, got], axis=1), jnp.concatenate([got, keep], axis=1)
    )
    return out[None], token_loss


def solution(mesh):
    placed = (P("rep", "tok", None), P("tok", "voc"), P("tok"), P("tok"))
    return jax.shard_map(
        shards,
        mesh=mesh,
        in_specs=placed,
        out_specs=(P("rep", ("tok", "voc"), None), P("rep", "tok")),
        check_vma=False,
    )
```

```python
import functools

import jax
import jax.numpy as jnp
from jax import lax
from jax.experimental import pallas as pl
from jax.experimental.pallas import tpu as pltpu
from jax.sharding import Mesh, PartitionSpec as P

softcap_limit = 30.0
kl_weight = 0.5
loss_scale = 16.0

N_Y, N_Z, N_C, N_X = 4, 8, 2, 4
LINE = ("rep", "tok")
ROWS = 192
QUARTER = 512
HALF_D = 1792
TILE = 256
VMEM = 50 * 1024 * 1024
F32, BF16 = jnp.float32, jnp.bfloat16


def line_xor(block, k):
    k = (k % 2) * 2 + k // 2
    return lax.ppermute(block, LINE, [(x, x ^ k) for x in range(N_X)])


def axis_xor(block, axis, k):
    return lax.ppermute(block, axis, [(i, i ^ k) for i in range(lax.axis_size(axis))])


def logits_kernel(at, own, nbr, far, head_a, head_b, got_a, got_b, tgt, logits, stats, rows, sums):
    step = pl.program_id(0)
    tok = at[0]

    @pl.when(step == 0)
    def _():
        for side in range(2):
            half = tok if side == 0 else 1 - tok
            begin = pl.multiple_of(half * HALF_D, HALF_D)
            to = pl.ds(side * HALF_D, HALF_D)
            rows[0:ROWS, to] = own[:, pl.ds(begin, HALF_D)]
            rows[ROWS : 2 * ROWS, to] = nbr[:, pl.ds(begin, HALF_D)]
            for part in range(2):
                rows[2 * ROWS :, pl.ds(side * HALF_D + part * 896, 896)] = far[
                    half * 2 + part
                ].reshape(2 * ROWS, 896)
        sums[...] = jnp.zeros_like(sums)

    def one(head, got, core):
        raw = jnp.dot(rows[:, :HALF_D], head[...], preferred_element_type=F32)
        raw = raw + jnp.dot(rows[:, HALF_D:], got[...], preferred_element_type=F32)
        capped = softcap_limit * jnp.tanh(raw * (1.0 / softcap_limit))
        far_part = capped[2 * ROWS :].reshape(8, 2, 24, TILE)
        blocks = [
            capped[:ROWS],
            capped[ROWS : 2 * ROWS],
            far_part[:, 0].reshape(ROWS, TILE),
            far_part[:, 1].reshape(ROWS, TILE),
        ]
        lane = lax.broadcasted_iota(jnp.int32, (ROWS, TILE), 1) + at[2 + core]
        for j in range(4):
            mine = blocks[j]
            shared = blocks[j ^ 1].astype(BF16).astype(F32)
            logits[j] = mine
            partner = jnp.exp(shared)
            hit = lane == tgt[j // 2]
            terms = (
                jnp.exp(mine),
                partner,
                jnp.where(hit, mine, 0.0),
                partner * (shared - mine),
            )
            for s, term in enumerate(terms):
                sums[s, j] += term[:, :128] + term[:, 128:]

    @pl.when(step == 0)
    def _():
        one(head_a, got_a, 0)

    @pl.when(step == 1)
    def _():
        one(head_b, got_b, 1)
        lane = lax.broadcasted_iota(jnp.int32, (ROWS, 128), 1)
        for j in range(4):
            wide = jnp.zeros((ROWS, 128), F32)
            for s in range(4):
                wide = jnp.where(lane == s, jnp.sum(sums[s, j], axis=1, keepdims=True), wide)
            wide = jnp.concatenate([wide, jnp.zeros((256 - ROWS, 128), F32)], axis=0)
            stats[j] = wide.T[:8]


def logits_call(at, own, nbr, far, head, mate, got, got_mate, tgt, part):
    def whole(*shape):
        return pl.BlockSpec(shape, lambda s, at: (0,) * len(shape))

    return pl.pallas_call(
        logits_kernel,
        grid_spec=pltpu.PrefetchScalarGridSpec(
            num_scalar_prefetch=1,
            grid=(2,),
            in_specs=[
                whole(ROWS, 2 * HALF_D),
                whole(ROWS, 2 * HALF_D),
                whole(4, 8, 48, 896),
                pl.BlockSpec((HALF_D, TILE), lambda s, at: (0, at[1] * 2 + part)),
                pl.BlockSpec((HALF_D, TILE), lambda s, at: (0, at[1] * 2 + part)),
                whole(HALF_D, TILE),
                whole(HALF_D, TILE),
                whole(2, ROWS, 1),
            ],
            out_specs=[
                pl.BlockSpec((4, ROWS, TILE), lambda s, at: (0, 0, s)),
                whole(4, 8, 256),
            ],
            scratch_shapes=[
                pltpu.VMEM((4 * ROWS, 2 * HALF_D), BF16),
                pltpu.VMEM((4, 4, ROWS, 128), F32),
            ],
        ),
        out_shape=[
            jax.ShapeDtypeStruct((4, ROWS, 2 * TILE), F32),
            jax.ShapeDtypeStruct((4, 8, 256), F32),
        ],
        compiler_params=pltpu.CompilerParams(vmem_limit_bytes=VMEM),
        cost_estimate=pl.CostEstimate(
            flops=4 * ROWS * 2 * TILE * 2 * HALF_D * 2, bytes_accessed=16 << 20, transcendentals=1 << 21
        ),
        name="logits",
    )(at, own, nbr, far, head, mate, got, got_mate, tgt)


def grad_kernel(at, first, second, stats, tgt, mask, mine, theirs, scales):
    step = pl.program_id(0)

    @pl.when(step == 0)
    def _():
        for j in range(4):
            total = stats[j].T
            weight = loss_scale * mask[j // 2]
            scales[0, j] = (1.0 + kl_weight) * weight / total[:ROWS, 0:1]
            scales[1, j] = kl_weight * weight / total[:ROWS, 1:2]

    core, part = step // 2, step % 2
    column = lax.broadcasted_iota(jnp.int32, (ROWS, TILE), 1)
    column = column + jnp.where(core == 0, at[2], at[3]) + part * TILE

    def work(logits):
        for j in range(4):
            own = logits[j]
            shared = logits[j ^ 1].astype(BF16).astype(F32)
            weight = loss_scale * mask[j // 2]
            hit = jnp.where(column == tgt[j // 2], weight, 0.0)
            slope = own * (1.0 / softcap_limit)
            value = jnp.exp(own) * scales[0, j] - hit - jnp.exp(shared) * scales[1, j]
            value = (value * (1.0 - slope * slope)).astype(BF16)
            if j % 2 == 0:
                mine[j // 2] = value
            else:
                theirs[j // 2] = value

    @pl.when(part == 0)
    def _():
        work(first)

    @pl.when(part == 1)
    def _():
        work(second)


def grad_call(at, first, second, stats, tgt, mask):
    def whole(*shape):
        return pl.BlockSpec(shape, lambda s, at: (0,) * len(shape))

    out = pl.BlockSpec((2, ROWS, TILE), lambda s, at: (0, 0, s))
    return pl.pallas_call(
        grad_kernel,
        grid_spec=pltpu.PrefetchScalarGridSpec(
            num_scalar_prefetch=1,
            grid=(4,),
            in_specs=[
                pl.BlockSpec((4, ROWS, TILE), lambda s, at: (0, 0, s // 2)),
                pl.BlockSpec((4, ROWS, TILE), lambda s, at: (0, 0, s // 2)),
                whole(4, 8, 256),
                whole(2, ROWS, 1),
                whole(2, ROWS, 1),
            ],
            out_specs=[out, out],
            scratch_shapes=[pltpu.VMEM((2, 4, ROWS, 1), F32)],
        ),
        out_shape=[jax.ShapeDtypeStruct((2, ROWS, 4 * TILE), BF16)] * 2,
        compiler_params=pltpu.CompilerParams(vmem_limit_bytes=VMEM),
        name="logit_grad",
    )(at, first, second, stats, tgt, mask)


def terms_kernel(at, grad, head, mate, *rest, order):
    acc, out = rest if len(rest) == 2 else (None, rest[0])
    contract = (((1,), (1,)), ((), ()))
    left = jnp.concatenate([grad[k] for k in order], axis=0)
    total = lax.dot_general(left[:, :QUARTER], head[...], contract, preferred_element_type=F32)
    total = total + lax.dot_general(left[:, QUARTER:], mate[...], contract, preferred_element_type=F32)
    if acc is not None:
        total = total + acc[...]
    out[...] = total


def terms_call(at, grad, head, mate, acc, k):
    order = (0, 1) if k < 2 else (1, 0)

    def weights(s, at):
        return (s, at[1] ^ k)

    tile = pl.BlockSpec((2 * ROWS, TILE), lambda s, at: (0, s))
    accs = [] if acc is None else [acc]
    return pl.pallas_call(
        functools.partial(terms_kernel, order=order),
        grid_spec=pltpu.PrefetchScalarGridSpec(
            num_scalar_prefetch=1,
            grid=(HALF_D // TILE,),
            in_specs=[
                pl.BlockSpec((2, ROWS, 4 * TILE), lambda s, at: (0, 0, 0)),
                pl.BlockSpec((TILE, QUARTER), weights),
                pl.BlockSpec((TILE, QUARTER), weights),
            ] + [tile] * len(accs),
            out_specs=tile,
        ),
        out_shape=jax.ShapeDtypeStruct((2 * ROWS, HALF_D), F32),
        compiler_params=pltpu.CompilerParams(vmem_limit_bytes=VMEM),
        cost_estimate=pl.CostEstimate(
            flops=2 * 2 * ROWS * HALF_D * 2 * QUARTER, bytes_accessed=8 << 20, transcendentals=0
        ),
        name="gradient_terms",
    )(at, grad, head, mate, *accs)


def add_over_slice(stats):
    for k in (1, 2):
        other = line_xor(stats, k)
        stats = stats + jnp.stack([other[j ^ k] for j in range(4)])
    for k in (1, 2):
        stats = stats + axis_xor(stats, "y", k)
    for k in (1, 2, 4):
        stats = stats + axis_xor(stats, "z", k)
    return stats


def pick_rows(block, count, core):
    out = lax.broadcasted_iota(jnp.int32, (count, 2 * count), 0)
    src = lax.broadcasted_iota(jnp.int32, (count, 2 * count), 1)
    pick = (src == out // 6 * 12 + core * 6 + out % 6).astype(BF16)
    return jnp.dot(pick, block, preferred_element_type=F32).astype(BF16)


def shards(hidden, head, targets, loss_mask):
    rep, tok, y, z, core = (lax.axis_index(a) for a in ("rep", "tok", "y", "z", "core"))
    x = tok * 2 + rep
    states = hidden[0]

    slab = pick_rows(lax.dynamic_slice(states, (z * 48, y * 896), (48, 896)), 24, core)
    piece = jnp.concatenate([line_xor(slab, 2), line_xor(slab, 3)], axis=0)[None]
    far = lax.all_gather(piece, ("y", "z"), axis=0, tiled=True).reshape(4, 8, 48, 896)

    got, got_mate = [], []
    for part in range(2):
        sent = lax.dynamic_slice(head, (0, (3 - x) * QUARTER + part * TILE), (HALF_D, TILE))
        got.append(line_xor(sent, 3))
        got_mate.append(axis_xor(got[-1], "core", 1))
    own = pick_rows(states, ROWS, core)
    nbr = line_xor(own, 1)
    mate = axis_xor(head, "core", 1)

    voc = (y * 8 + z) * 2
    begin = [(voc + c) * 2048 + x * QUARTER for c in (core, 1 - core)]
    scal = jnp.stack([targets, loss_mask]).reshape(2, 32, 2, 6)
    scal = lax.dynamic_index_in_dim(scal, core, 2, keepdims=False).reshape(2, ROWS)
    scal = jnp.stack([scal, line_xor(scal, 2)], axis=1)[..., None]
    tgt, mask = scal[0], scal[1].astype(F32)

    parts = []
    for part in range(2):
        at = jnp.stack([tok, x, begin[0] + part * TILE, begin[1] + part * TILE]).astype(jnp.int32)
        parts.append(
            logits_call(at, own, nbr, far, head, mate, got[part], got_mate[part], tgt, part)
        )
    at = jnp.stack([tok, x, begin[0], begin[1]]).astype(jnp.int32)
    stats = add_over_slice(parts[0][1] + parts[1][1])

    mine, theirs = grad_call(at, parts[0][0], parts[1][0], stats, tgt, mask)
    grads = [mine, line_xor(theirs, 1), line_xor(mine, 2), line_xor(theirs, 3)]
    terms = None
    for k, grad in enumerate(grads):
        terms = terms_call(at, grad, head, mate, terms, k)

    own_total, partner_total, picked, cross = (stats[0, s, :ROWS] for s in range(4))
    own_lse, partner_lse = jnp.log(own_total), jnp.log(partner_total)
    loss = mask[0, :, 0] * (
        own_lse - picked + kl_weight * (cross / partner_total - partner_lse + own_lse)
    )
    pair = jnp.stack([loss, axis_xor(loss, "core", 1)]).reshape(2, 32, 6)
    pair = jnp.where(core == 0, pair, pair[::-1])
    token_loss = pair.transpose(1, 0, 2).reshape(1, 384)

    terms = terms.reshape(2, 4, 48, HALF_D)
    low = terms.astype(BF16)

    def part_of(array, at, axis):
        return lax.dynamic_index_in_dim(array, at, axis, keepdims=False)

    total = part_of(terms, y, 1)
    for other in [axis_xor(part_of(low, y ^ k, 1), "y", k) for k in (1, 2, 3)]:
        total = total + other.astype(F32)
    out = lax.broadcasted_iota(jnp.int32, (128, 96), 0)
    src = lax.broadcasted_iota(jnp.int32, (128, 96), 1)
    wanted = (out // 8 % 2) * 48 + out // 16 * 6 + out % 8
    pick = ((src == wanted) & (out % 8 < 6)).astype(BF16)
    low = jnp.dot(pick, total.reshape(96, HALF_D).astype(BF16), preferred_element_type=F32)
    low = low.astype(BF16).reshape(8, 16, HALF_D)
    total = part_of(low, z, 0).astype(F32)
    for other in [axis_xor(part_of(low, z ^ k, 0), "z", k) for k in range(1, 8)]:
        total = total + other.astype(F32)
    total = total.astype(BF16).reshape(2, 8, HALF_D)
    got = line_xor(total[1], 2)[:6]
    keep = total[0, :6]
    out = jnp.where(
        tok == 0, jnp.concatenate([keep, got], axis=1), jnp.concatenate([got, keep], axis=1)
    )
    return out[None], token_loss


def solution(mesh):
    fine = Mesh(
        mesh.devices.reshape(2, 2, N_Y, N_Z, N_C), ("rep", "tok", "y", "z", "core")
    )
    voc = ("y", "z", "core")
    placed = (P("rep", "tok", None), P("tok", voc), P("tok"), P("tok"))
    return jax.shard_map(
        shards,
        mesh=fine,
        in_specs=placed,
        out_specs=(P("rep", ("tok", *voc), None), P("rep", "tok")),
        check_vma=False,
    )
```

```python
import functools

import jax
import jax.numpy as jnp
from jax import lax
from jax.experimental import pallas as pl
from jax.experimental.pallas import tpu as pltpu
from jax.sharding import Mesh, PartitionSpec as P

softcap_limit = 30.0
kl_weight = 0.5
loss_scale = 16.0

N_Y, N_Z, N_C, N_X = 4, 8, 2, 4
LINE = ("rep", "tok")
ROWS = 192
QUARTER = 512
HALF_D = 1792
CHUNKS = (256, 256, 640, 640)
TILE = 256
VMEM = 50 * 1024 * 1024
F32, BF16 = jnp.float32, jnp.bfloat16


def line_xor(block, k):
    k = (k % 2) * 2 + k // 2
    return lax.ppermute(block, LINE, [(x, x ^ k) for x in range(N_X)])


def axis_xor(block, axis, k):
    return lax.ppermute(block, axis, [(i, i ^ k) for i in range(lax.axis_size(axis))])


def whole(*shape):
    return pl.BlockSpec(shape, lambda s, at: (0,) * len(shape))


def logits_kernel(at, own, nbr_a, nbr_b, *refs):
    far, head, mate, got, tgt = refs[:4], refs[4], refs[5], refs[6:14], refs[14]
    logits, stats, rows, raw, sums = refs[15:]
    step = pl.program_id(0)
    tok, y, z = at[0], at[2], at[3]

    @pl.when(step == 0)
    def _():
        for side in range(2):
            half = tok if side == 0 else 1 - tok
            begin = pl.multiple_of(half * HALF_D, 128)
            to = pl.ds(side * HALF_D, HALF_D)
            rows[0:ROWS, to] = own[:, pl.ds(begin, HALF_D)]
            rows[ROWS : ROWS + 96, to] = nbr_a[:, pl.ds(begin, HALF_D)]
            rows[ROWS + 96 : 2 * ROWS, to] = nbr_b[:, pl.ds(begin, HALF_D)]
        for k in range(4):
            d = y ^ k
            column = pl.multiple_of((d // 2 ^ tok) * HALF_D + d % 2 * 896, 128)
            for s in range(8):
                row = 2 * ROWS + (z ^ s) * 48
                rows[pl.ds(pl.multiple_of(row, 16), 48), pl.ds(column, 896)] = far[k][s]
        sums[...] = jnp.zeros_like(sums)

    lane = lax.broadcasted_iota(jnp.int32, (48, TILE), 1)

    def one(head, got, part, core):
        total = jnp.dot(rows[:, :HALF_D], head[...], preferred_element_type=F32)
        begin = HALF_D
        for count, chunk in zip(CHUNKS, got):
            total = total + jnp.dot(
                rows[:, begin : begin + count], chunk[...], preferred_element_type=F32
            )
            begin += count
        raw[...] = total
        column = lane + (at[4 + core] + part * TILE)
        for chunk in range(8):
            pair, g = chunk // 4, chunk % 4
            here = slice(g * 48, g * 48 + 48)
            if pair == 0:
                both = [raw[here], raw[ROWS + g * 48 : ROWS + g * 48 + 48]]
            else:
                begin = 2 * ROWS + g * 96
                pieces = [raw[begin + 24 * i : begin + 24 * i + 24] for i in range(4)]
                both = [jnp.concatenate(pieces[i::2], axis=0) for i in range(2)]
            both = [softcap_limit * jnp.tanh(v * (1.0 / softcap_limit)) for v in both]
            target = tgt[pair, here]
            hit = column == jnp.concatenate([target, target], axis=1)
            shared = [v.astype(BF16).astype(F32) for v in both]
            partner = [jnp.exp(v) for v in shared]
            for i in range(2):
                j = pair * 2 + i
                mine = both[i]
                logits[j, here] = mine
                terms = (
                    jnp.exp(mine),
                    partner[1 - i],
                    jnp.where(hit, mine, 0.0),
                    partner[1 - i] * (shared[1 - i] - mine),
                )
                for s, term in enumerate(terms):
                    sums[s, j, here] += term[:, :128] + term[:, 128:]

    for part in range(2):
        for core in range(2):
            @pl.when(step == part * 2 + core)
            def _(part=part, core=core):
                one((head, mate)[core], got[core * 4 : core * 4 + 4], part, core)

    @pl.when(step == 3)
    def _():
        lane = lax.broadcasted_iota(jnp.int32, (ROWS, 128), 1)
        for j in range(4):
            wide = jnp.zeros((ROWS, 128), F32)
            for s in range(4):
                wide = jnp.where(lane == s, jnp.sum(sums[s, j], axis=1, keepdims=True), wide)
            wide = jnp.concatenate([wide, jnp.zeros((256 - ROWS, 128), F32)], axis=0)
            stats[at[1] ^ j] = wide.T[:8]


def logits_call(at, own, nbr, far, head, mate, got, tgt):
    weights = pl.BlockSpec((HALF_D, TILE), lambda s, at: (0, at[1] * 2 + s // 2))
    return pl.pallas_call(
        logits_kernel,
        grid_spec=pltpu.PrefetchScalarGridSpec(
            num_scalar_prefetch=1,
            grid=(4,),
            in_specs=[whole(ROWS, 2 * HALF_D)]
            + [whole(ROWS // 2, 2 * HALF_D)] * 2
            + [whole(8, 48, 896)] * 4
            + [weights, pl.BlockSpec((HALF_D, TILE), lambda s, at: (0, s // 2))]
            + [pl.BlockSpec((c, TILE), lambda s, at: (0, s // 2)) for c in CHUNKS] * 2
            + [whole(2, ROWS, 128)],
            out_specs=[
                pl.BlockSpec((4, ROWS, TILE), lambda s, at: (0, 0, s % 2 * 2 + s // 2)),
                whole(4, 8, 256),
            ],
            scratch_shapes=[
                pltpu.VMEM((4 * ROWS, 2 * HALF_D), BF16),
                pltpu.VMEM((4 * ROWS, TILE), F32),
                pltpu.VMEM((4, 4, ROWS, 128), F32),
            ],
        ),
        out_shape=[
            jax.ShapeDtypeStruct((4, ROWS, 4 * TILE), F32),
            jax.ShapeDtypeStruct((4, 8, 256), F32),
        ],
        compiler_params=pltpu.CompilerParams(vmem_limit_bytes=VMEM),
        cost_estimate=pl.CostEstimate(
            flops=4 * ROWS * 4 * TILE * 2 * HALF_D * 2, bytes_accessed=16 << 20, transcendentals=1 << 21
        ),
        name="logits",
    )(at, own, *nbr, *far, head, mate, *got, tgt)


def grad_kernel(at, logits, stats, tgt, mask, mine, theirs, scales):
    step = pl.program_id(0)

    @pl.when(step == 0)
    def _():
        for j in range(4):
            total = stats[at[1] ^ j].T
            weight = loss_scale * mask[j // 2]
            scales[0, j] = (1.0 + kl_weight) * weight / total[:ROWS, 0:1]
            scales[1, j] = kl_weight * weight / total[:ROWS, 1:2]

    core, part = step // 2, step % 2
    column = lax.broadcasted_iota(jnp.int32, (48, TILE), 1)
    column = column + (jnp.where(core == 0, at[4], at[5]) + part * TILE)

    for pair in range(2):
        for g in range(4):
            here = slice(g * 48, g * 48 + 48)
            both = [logits[pair * 2, here], logits[pair * 2 + 1, here]]
            target, weight = tgt[pair, here], loss_scale * mask[pair, here]
            target = jnp.concatenate([target, target], axis=1)
            weight = jnp.concatenate([weight, weight], axis=1)
            hit = jnp.where(column == target, weight, 0.0)
            for i in range(2):
                own = both[i]
                shared = both[1 - i].astype(BF16).astype(F32)
                own_scale, partner_scale = (
                    jnp.concatenate([scales[n, pair * 2 + i, here]] * 2, axis=1) for n in range(2)
                )
                slope = own * (1.0 / softcap_limit)
                value = jnp.exp(own) * own_scale - hit - jnp.exp(shared) * partner_scale
                (mine, theirs)[i][pair, here] = (value * (1.0 - slope * slope)).astype(BF16)


def grad_call(at, logits, stats, tgt, mask):
    out = pl.BlockSpec((2, ROWS, TILE), lambda s, at: (0, 0, s))
    return pl.pallas_call(
        grad_kernel,
        grid_spec=pltpu.PrefetchScalarGridSpec(
            num_scalar_prefetch=1,
            grid=(4,),
            in_specs=[
                pl.BlockSpec((4, ROWS, TILE), lambda s, at: (0, 0, s)),
                whole(4, 8, 256),
                whole(2, ROWS, 128),
                whole(2, ROWS, 128),
            ],
            out_specs=[out, out],
            scratch_shapes=[pltpu.VMEM((2, 4, ROWS, 128), F32)],
        ),
        out_shape=[jax.ShapeDtypeStruct((2, ROWS, 4 * TILE), BF16)] * 2,
        compiler_params=pltpu.CompilerParams(vmem_limit_bytes=VMEM),
        name="logit_grad",
    )(at, logits, stats, tgt, mask)


def terms_kernel(at, *refs, ks, last):
    refs = list(refs)
    total = None
    for k in ks:
        grad, head, mate = refs[:3]
        refs = refs[3:]
        order = (0, 1) if k < 2 else (1, 0)
        for core, weight in enumerate((head, mate)):
            begin = core * QUARTER
            left = jnp.concatenate([grad[t, :, begin : begin + QUARTER] for t in order], axis=0)
            term = jnp.dot(left, weight[...], preferred_element_type=F32)
            total = term if total is None else total + term
    if not last:
        refs[0][...] = total
        return
    total = total + refs[0][...]
    outs, scratch = refs[1:5], refs[5]
    for tok in range(2):
        for y in range(4):
            begin = tok * ROWS + y * 48
            scratch[y, tok] = total[begin : begin + 48]
    for k in range(4):
        outs[k][...] = scratch[at[2] ^ k].astype(outs[k].dtype)


def terms_call(at, grads, head, mate, ks, acc=None):
    last = acc is not None
    tile = pl.BlockSpec((2 * ROWS, TILE), lambda s, at: (0, s))
    in_specs, args = [], []
    for k, grad in zip(ks, grads):
        weights = pl.BlockSpec((QUARTER, TILE), lambda s, at, k=k: (at[1] ^ k, s))
        in_specs += [pl.BlockSpec((2, ROWS, 4 * TILE), lambda s, at: (0, 0, 0)), weights, weights]
        args += [grad, head, mate]
    out_specs, scratch = tile, []
    out_shape = jax.ShapeDtypeStruct((2 * ROWS, HALF_D), F32)
    if last:
        in_specs.append(tile)
        args.append(acc)
        out_specs = [pl.BlockSpec((2, 48, TILE), lambda s, at: (0, 0, s))] * 4
        out_shape = [jax.ShapeDtypeStruct((2, 48, HALF_D), t) for t in (F32, BF16, BF16, BF16)]
        scratch = [pltpu.VMEM((4, 2, 48, TILE), F32)]
    return pl.pallas_call(
        functools.partial(terms_kernel, ks=ks, last=last),
        grid_spec=pltpu.PrefetchScalarGridSpec(
            num_scalar_prefetch=1,
            grid=(HALF_D // TILE,),
            in_specs=in_specs,
            out_specs=out_specs,
            scratch_shapes=scratch,
        ),
        out_shape=out_shape,
        compiler_params=pltpu.CompilerParams(vmem_limit_bytes=VMEM),
        cost_estimate=pl.CostEstimate(
            flops=2 * 2 * ROWS * HALF_D * 2 * QUARTER * len(ks),
            bytes_accessed=(6 << 20) * len(ks),
            transcendentals=0,
        ),
        name="gradient_terms",
    )(at, *args)


def rows_kernel(at, *refs):
    parts, outs = refs[:4], refs[4:]
    total = parts[0][...]
    for part in parts[1:]:
        total = total + part[...].astype(F32)
    z = at[3]
    out = lax.broadcasted_iota(jnp.int32, (128, 96), 0)
    src = lax.broadcasted_iota(jnp.int32, (128, 96), 1)
    owner = ((z >> 1) ^ ((out >> 3) & 3)) * 2 + ((z ^ (out >> 6)) & 1)
    i = out & 7
    wanted = ((out >> 5) & 1) * 48 + owner * 6 + i
    pick = jnp.where((src == wanted) & (i < 6), 1.0, 0.0).astype(BF16)
    low = jnp.dot(pick, total.reshape(96, 896).astype(BF16), preferred_element_type=F32)
    for n in range(4):
        outs[n][...] = low[n * 32 : n * 32 + 32].astype(BF16)


def rows_call(at, parts):
    return pl.pallas_call(
        rows_kernel,
        grid_spec=pltpu.PrefetchScalarGridSpec(
            num_scalar_prefetch=1,
            grid=(2,),
            in_specs=[pl.BlockSpec((2, 48, 896), lambda s, at: (0, 0, s))] * 4,
            out_specs=[pl.BlockSpec((32, 896), lambda s, at: (0, s))] * 4,
        ),
        out_shape=[jax.ShapeDtypeStruct((32, HALF_D), BF16)] * 4,
        compiler_params=pltpu.CompilerParams(vmem_limit_bytes=VMEM),
        name="rows",
    )(at, *parts)


def half_kernel(at, *refs):
    parts, first, others, scratch = refs[:4], refs[4], refs[5:8], refs[8]
    for side in range(2):
        half = parts[2 * side][...].astype(F32) + parts[2 * side + 1][...].astype(F32)
        begin = (at[0] ^ side) * HALF_D
        scratch[:, pl.ds(pl.multiple_of(begin, 128), HALF_D)] = half
    first[...] = scratch[0:8]
    for m in range(1, 4):
        others[m - 1][...] = scratch[m * 8 : m * 8 + 8].astype(BF16)


def half_call(at, parts):
    return pl.pallas_call(
        half_kernel,
        grid_spec=pltpu.PrefetchScalarGridSpec(
            num_scalar_prefetch=1,
            grid=(1,),
            in_specs=[whole(32, HALF_D)] * 4,
            out_specs=[whole(8, 2 * HALF_D)] * 4,
            scratch_shapes=[pltpu.VMEM((32, 2 * HALF_D), F32)],
        ),
        out_shape=[jax.ShapeDtypeStruct((8, 2 * HALF_D), t) for t in (F32, BF16, BF16, BF16)],
        name="half",
    )(at, *parts)


def tree_sum(values):
    values = list(values)
    while len(values) > 1:
        values = [a + b for a, b in zip(values[::2], values[1::2])]
    return values[0]


def add_over_slice(stats):
    stats = tree_sum([stats] + [line_xor(stats, k) for k in (1, 2, 3)])
    stats = tree_sum([stats] + [axis_xor(stats, "y", k) for k in (1, 2, 3)])
    return tree_sum([stats] + [axis_xor(stats, "z", k) for k in range(1, 8)])


def pick_rows(block, count, core):
    out = lax.broadcasted_iota(jnp.int32, (count, 2 * count), 0)
    src = lax.broadcasted_iota(jnp.int32, (count, 2 * count), 1)
    pick = (src == out // 6 * 12 + core * 6 + out % 6).astype(BF16)
    return jnp.dot(pick, block, preferred_element_type=F32).astype(BF16)


def shards(hidden, head, targets, loss_mask):
    rep, tok, y, z, core = (lax.axis_index(a) for a in ("rep", "tok", "y", "z", "core"))
    x = tok * 2 + rep
    states = hidden[0]

    sync = lax.optimization_barrier

    def chunk(n):
        return lax.dynamic_slice(head, (sum(CHUNKS[:n]), (3 - x) * QUARTER), (CHUNKS[n], QUARTER))

    got = []
    slab = pick_rows(lax.dynamic_slice(states, (z * 48, y * 896), (48, 896)), 24, core)
    got.append(line_xor(chunk(0), 3))
    slabs = [line_xor(slab, 2), line_xor(slab, 3)]
    piece = jnp.concatenate(slabs, axis=0)
    piece, got[0], head, states = sync((piece, got[0], head, states))

    got.append(line_xor(chunk(1), 3))
    far = jnp.concatenate([piece[None], axis_xor(piece[None], "z", 1)])
    own = pick_rows(states, ROWS, core)
    far, got[1], head, own = sync((far, got[1], head, own))

    voc = (y * 8 + z) * 2
    begin = [(voc + c) * 2048 + x * QUARTER for c in (core, 1 - core)]
    at = jnp.stack([tok, x, y, z, begin[0], begin[1]]).astype(jnp.int32)
    scal = jnp.stack([targets, loss_mask]).reshape(2, 32, 2, 6)
    scal = lax.dynamic_index_in_dim(scal, core, 2, keepdims=False).reshape(2, ROWS)

    got.append(line_xor(chunk(2), 3))
    nbr = [line_xor(own[:96], 1)]
    far = jnp.concatenate([far] + [axis_xor(far, "z", k) for k in (2, 4, 6)])
    mate = axis_xor(lax.dynamic_slice(head, (0, x * QUARTER), (HALF_D, QUARTER)), "core", 1)
    got_mate = [axis_xor(got[0], "core", 1)]
    scal = jnp.stack([scal, line_xor(scal, 2)], axis=1)
    mask = scal[1].astype(F32)
    tgt_wide = jnp.broadcast_to(scal[0][..., None], (2, ROWS, 128))
    mask_wide = jnp.broadcast_to(mask[..., None], (2, ROWS, 128))
    far, got[2], nbr[0], head, own, mate, got_mate[0], tgt_wide, mask_wide = sync(
        (far, got[2], nbr[0], head, own, mate, got_mate[0], tgt_wide, mask_wide)
    )

    got.append(line_xor(chunk(3), 3))
    nbr.append(line_xor(own[96:], 1))
    far = [far] + [axis_xor(far, "y", k) for k in (1, 2, 3)]
    got_mate += [axis_xor(got[n], "core", 1) for n in (1, 2)]
    head_t = head.T
    head_t, got[3], nbr[1], *far = sync((head_t, got[3], nbr[1], *far))
    got_mate.append(axis_xor(got[3], "core", 1))
    got = got + got_mate

    logits, stats = logits_call(at, own, nbr, far, head, mate, got, tgt_wide)
    head_t, stats = sync((head_t, stats))
    mate_t = axis_xor(head_t, "core", 1)
    stats = add_over_slice(stats)

    mine, theirs = grad_call(at, logits, stats, tgt_wide, mask_wide)
    grads = [mine, line_xor(theirs, 1), line_xor(mine, 2), line_xor(theirs, 3)]
    terms = terms_call(at, grads[:1], head_t, mate_t, (0,))
    parts = list(terms_call(at, grads[1:], head_t, mate_t, (1, 2, 3), terms))

    stats, parts[0] = sync((stats, parts[0]))
    stats = lax.dynamic_index_in_dim(stats, x, 0, keepdims=False)
    own_total, partner_total, picked, cross = (stats[s, :ROWS] for s in range(4))
    own_lse, partner_lse = jnp.log(own_total), jnp.log(partner_total)
    loss = mask[0] * (
        own_lse - picked + kl_weight * (cross / partner_total - partner_lse + own_lse)
    )
    pair = jnp.stack([loss, axis_xor(loss, "core", 1)]).reshape(2, 32, 6)
    pair = jnp.where(core == 0, pair, pair[::-1])
    token_loss = pair.transpose(1, 0, 2).reshape(1, 384)

    parts = [parts[0]] + [axis_xor(parts[k], "y", k) for k in (1, 2, 3)]
    token_loss, parts[0] = sync((token_loss, parts[0]))
    parts = rows_call(at, parts)
    parts = [
        parts[0],
        axis_xor(parts[2], "z", 1),
        line_xor(parts[1], 2),
        lax.ppermute(parts[3], ("tok", "z"), [(i, i ^ 9) for i in range(16)]),
    ]
    parts = half_call(at, parts)
    total = parts[0]
    for m in (1, 2, 3):
        total = total + axis_xor(parts[m], "z", 2 * m).astype(F32)
    return total[:6].astype(BF16)[None], token_loss


def solution(mesh):
    fine = Mesh(
        mesh.devices.reshape(2, 2, N_Y, N_Z, N_C), ("rep", "tok", "y", "z", "core")
    )
    voc = ("y", "z", "core")
    placed = (P("rep", "tok", None), P("tok", voc), P("tok"), P("tok"))
    return jax.shard_map(
        shards,
        mesh=fine,
        in_specs=placed,
        out_specs=(P("rep", ("tok", *voc), None), P("rep", "tok")),
        check_vma=False,
    )
```

```python
import functools

import jax
import jax.numpy as jnp
from jax import lax
from jax.experimental import pallas as pl
from jax.experimental.pallas import tpu as pltpu
from jax.sharding import Mesh, PartitionSpec as P

softcap_limit = 30.0
kl_weight = 0.5
loss_scale = 16.0

N_Y, N_Z, N_C, N_X = 4, 8, 2, 4
LINE = ("rep", "tok")
ROWS = 192
QUARTER = 512
HALF_D = 1792
CHUNKS = (896, 896)
TILE = 256
VMEM = 50 * 1024 * 1024
F32, BF16 = jnp.float32, jnp.bfloat16


def line_xor(block, k):
    k = (k % 2) * 2 + k // 2
    return lax.ppermute(block, LINE, [(x, x ^ k) for x in range(N_X)])


def axis_xor(block, axis, k):
    return lax.ppermute(block, axis, [(i, i ^ k) for i in range(lax.axis_size(axis))])


def whole(*shape):
    return pl.BlockSpec(shape, lambda s, at: (0,) * len(shape))


def logits_kernel(at, own, nbr_a, nbr_b, *refs):
    far, head, mate, got, tgt = refs[0], refs[1], refs[2], refs[3:7], refs[7]
    logits, stats, rows, raw, sums = refs[8:]
    step = pl.program_id(0)
    tok, y = at[0], at[2]

    @pl.when(step == 0)
    def _():
        for side in range(2):
            half = tok if side == 0 else 1 - tok
            begin = pl.multiple_of(half * HALF_D, 128)
            to = pl.ds(side * HALF_D, HALF_D)
            rows[0:ROWS, to] = own[:, pl.ds(begin, HALF_D)]
            rows[ROWS : ROWS + 96, to] = nbr_a[:, pl.ds(begin, HALF_D)]
            rows[ROWS + 96 : 2 * ROWS, to] = nbr_b[:, pl.ds(begin, HALF_D)]
        for k in range(4):
            d = y ^ k
            column = pl.multiple_of((d // 2 ^ tok) * HALF_D + d % 2 * 896, 128)
            rows[2 * ROWS :, pl.ds(column, 896)] = far[:, k].reshape(2 * ROWS, 896)
        sums[...] = jnp.zeros_like(sums)

    lane = lax.broadcasted_iota(jnp.int32, (48, TILE), 1)

    def one(head, got, part, core):
        weights = jnp.concatenate([head[...]] + [chunk[...] for chunk in got], axis=0)
        raw[...] = jnp.dot(rows[...], weights, preferred_element_type=F32)
        column = lane + (at[4 + core] + part * TILE)
        for chunk in range(8):
            pair, g = chunk // 4, chunk % 4
            here = slice(g * 48, g * 48 + 48)
            if pair == 0:
                both = [raw[here], raw[ROWS + g * 48 : ROWS + g * 48 + 48]]
            else:
                begin = 2 * ROWS + g * 96
                pieces = [raw[begin + 24 * i : begin + 24 * i + 24] for i in range(4)]
                both = [jnp.concatenate(pieces[i::2], axis=0) for i in range(2)]
            both = [softcap_limit * jnp.tanh(v * (1.0 / softcap_limit)) for v in both]
            target = tgt[pair, here]
            hit = column == jnp.concatenate([target, target], axis=1)
            shared = [v.astype(BF16).astype(F32) for v in both]
            partner = [jnp.exp(v) for v in shared]
            for i in range(2):
                j = pair * 2 + i
                mine = both[i]
                logits[j, here] = mine
                terms = (
                    jnp.exp(mine),
                    partner[1 - i],
                    jnp.where(hit, mine, 0.0),
                    partner[1 - i] * (shared[1 - i] - mine),
                )
                for s, term in enumerate(terms):
                    sums[s, j, here] += term[:, :128] + term[:, 128:]

    for part in range(2):
        for core in range(2):
            @pl.when(step == part * 2 + core)
            def _(part=part, core=core):
                one((head, mate)[core], got[core * 2 : core * 2 + 2], part, core)

    @pl.when(step == 3)
    def _():
        lane = lax.broadcasted_iota(jnp.int32, (ROWS, 128), 1)
        for j in range(4):
            wide = jnp.zeros((ROWS, 128), F32)
            for s in range(4):
                wide = jnp.where(lane == s, jnp.sum(sums[s, j], axis=1, keepdims=True), wide)
            wide = jnp.concatenate([wide, jnp.zeros((256 - ROWS, 128), F32)], axis=0)
            stats[at[1] ^ j] = wide.T[:8]


def logits_call(at, own, nbr, far, head, mate, got, tgt):
    weights = pl.BlockSpec((HALF_D, TILE), lambda s, at: (0, at[1] * 2 + s // 2))
    return pl.pallas_call(
        logits_kernel,
        grid_spec=pltpu.PrefetchScalarGridSpec(
            num_scalar_prefetch=1,
            grid=(4,),
            in_specs=[whole(ROWS, 2 * HALF_D)]
            + [whole(ROWS // 2, 2 * HALF_D)] * 2
            + [whole(8, 4, 48, 896)]
            + [weights, pl.BlockSpec((HALF_D, TILE), lambda s, at: (0, s // 2))]
            + [pl.BlockSpec((c, TILE), lambda s, at: (0, s // 2)) for c in CHUNKS] * 2
            + [whole(2, ROWS, 128)],
            out_specs=[
                pl.BlockSpec((4, ROWS, TILE), lambda s, at: (0, 0, s % 2 * 2 + s // 2)),
                whole(4, 8, 256),
            ],
            scratch_shapes=[
                pltpu.VMEM((4 * ROWS, 2 * HALF_D), BF16),
                pltpu.VMEM((4 * ROWS, TILE), F32),
                pltpu.VMEM((4, 4, ROWS, 128), F32),
            ],
        ),
        out_shape=[
            jax.ShapeDtypeStruct((4, ROWS, 4 * TILE), F32),
            jax.ShapeDtypeStruct((4, 8, 256), F32),
        ],
        compiler_params=pltpu.CompilerParams(vmem_limit_bytes=VMEM),
        cost_estimate=pl.CostEstimate(
            flops=4 * ROWS * 4 * TILE * 2 * HALF_D * 2, bytes_accessed=16 << 20, transcendentals=1 << 21
        ),
        name="logits",
    )(at, own, *nbr, far, head, mate, *got, tgt)


def grad_kernel(at, logits, stats, tgt, mask, mine, theirs, scales):
    step = pl.program_id(0)

    @pl.when(step == 0)
    def _():
        for j in range(4):
            total = stats[at[1] ^ j].T
            weight = loss_scale * mask[j // 2]
            scales[0, j] = (1.0 + kl_weight) * weight / total[:ROWS, 0:1]
            scales[1, j] = kl_weight * weight / total[:ROWS, 1:2]

    core, part = step // 2, step % 2
    column = lax.broadcasted_iota(jnp.int32, (48, TILE), 1)
    column = column + (jnp.where(core == 0, at[4], at[5]) + part * TILE)

    for pair in range(2):
        for g in range(4):
            here = slice(g * 48, g * 48 + 48)
            both = [logits[pair * 2, here], logits[pair * 2 + 1, here]]
            target, weight = tgt[pair, here], loss_scale * mask[pair, here]
            target = jnp.concatenate([target, target], axis=1)
            weight = jnp.concatenate([weight, weight], axis=1)
            hit = jnp.where(column == target, weight, 0.0)
            for i in range(2):
                own = both[i]
                shared = both[1 - i].astype(BF16).astype(F32)
                own_scale, partner_scale = (
                    jnp.concatenate([scales[n, pair * 2 + i, here]] * 2, axis=1) for n in range(2)
                )
                slope = own * (1.0 / softcap_limit)
                value = jnp.exp(own) * own_scale - hit - jnp.exp(shared) * partner_scale
                (mine, theirs)[i][pair, here] = (value * (1.0 - slope * slope)).astype(BF16)


def grad_call(at, logits, stats, tgt, mask):
    out = pl.BlockSpec((2, ROWS, TILE), lambda s, at: (0, 0, s))
    return pl.pallas_call(
        grad_kernel,
        grid_spec=pltpu.PrefetchScalarGridSpec(
            num_scalar_prefetch=1,
            grid=(4,),
            in_specs=[
                pl.BlockSpec((4, ROWS, TILE), lambda s, at: (0, 0, s)),
                whole(4, 8, 256),
                whole(2, ROWS, 128),
                whole(2, ROWS, 128),
            ],
            out_specs=[out, out],
            scratch_shapes=[pltpu.VMEM((2, 4, ROWS, 128), F32)],
        ),
        out_shape=[jax.ShapeDtypeStruct((2, ROWS, 4 * TILE), BF16)] * 2,
        compiler_params=pltpu.CompilerParams(vmem_limit_bytes=VMEM),
        name="logit_grad",
    )(at, logits, stats, tgt, mask)


def terms_kernel(at, *refs, ks, add, last):
    refs = list(refs)
    left, right = [], []
    for k in ks:
        grad, head, mate = refs[:3]
        refs = refs[3:]
        order = (0, 1) if k < 2 else (1, 0)
        left.append(jnp.concatenate([grad[t] for t in order], axis=0))
        right += [head[...], mate[...]]
    total = jnp.dot(
        jnp.concatenate(left, axis=1),
        jnp.concatenate(right, axis=0),
        preferred_element_type=F32,
    )
    if add:
        total = total + refs.pop(0)[...]
    if not last:
        refs[0][...] = total
        return
    outs, scratch = refs[:4], refs[4]
    for tok in range(2):
        for y in range(4):
            begin = tok * ROWS + y * 48
            scratch[y, tok] = total[begin : begin + 48]
    for k in range(4):
        outs[k][...] = scratch[at[2] ^ k].astype(outs[k].dtype)


def terms_call(at, grads, head, mate, ks, acc=None, last=False):
    tile = pl.BlockSpec((2 * ROWS, TILE), lambda s, at: (0, s))
    in_specs, args = [], []
    for k, grad in zip(ks, grads):
        weights = pl.BlockSpec((QUARTER, TILE), lambda s, at, k=k: (at[1] ^ k, s))
        in_specs += [pl.BlockSpec((2, ROWS, 4 * TILE), lambda s, at: (0, 0, 0)), weights, weights]
        args += [grad, head, mate]
    out_specs, scratch = tile, []
    out_shape = jax.ShapeDtypeStruct((2 * ROWS, HALF_D), F32)
    if acc is not None:
        in_specs.append(tile)
        args.append(acc)
    if last:
        out_specs = [pl.BlockSpec((2, 48, TILE), lambda s, at: (0, 0, s))] * 4
        out_shape = [jax.ShapeDtypeStruct((2, 48, HALF_D), t) for t in (F32, BF16, BF16, BF16)]
        scratch = [pltpu.VMEM((4, 2, 48, TILE), F32)]
    return pl.pallas_call(
        functools.partial(terms_kernel, ks=ks, add=acc is not None, last=last),
        grid_spec=pltpu.PrefetchScalarGridSpec(
            num_scalar_prefetch=1,
            grid=(HALF_D // TILE,),
            in_specs=in_specs,
            out_specs=out_specs,
            scratch_shapes=scratch,
        ),
        out_shape=out_shape,
        compiler_params=pltpu.CompilerParams(vmem_limit_bytes=VMEM),
        cost_estimate=pl.CostEstimate(
            flops=2 * 2 * ROWS * HALF_D * 2 * QUARTER * len(ks),
            bytes_accessed=(6 << 20) * len(ks),
            transcendentals=0,
        ),
        name="gradient_terms",
    )(at, *args)


def rows_kernel(at, *refs):
    parts, out_ref = refs[:4], refs[4]
    total = parts[0][...]
    for part in parts[1:]:
        total = total + part[...].astype(F32)
    out = lax.broadcasted_iota(jnp.int32, (128, 96), 0)
    src = lax.broadcasted_iota(jnp.int32, (128, 96), 1)
    i = out & 7
    wanted = ((out >> 6) ^ at[0]) * 48 + ((out >> 3) & 7) * 6 + i
    pick = jnp.where((src == wanted) & (i < 6), 1.0, 0.0).astype(BF16)
    low = jnp.dot(pick, total.reshape(96, 896).astype(BF16), preferred_element_type=F32)
    out_ref[...] = low.reshape(16, 8, 896).astype(BF16)


def rows_call(at, parts):
    return pl.pallas_call(
        rows_kernel,
        grid_spec=pltpu.PrefetchScalarGridSpec(
            num_scalar_prefetch=1,
            grid=(2,),
            in_specs=[pl.BlockSpec((2, 48, 896), lambda s, at: (0, 0, s))] * 4,
            out_specs=pl.BlockSpec((16, 8, 896), lambda s, at: (0, 0, s)),
        ),
        out_shape=jax.ShapeDtypeStruct((16, 8, HALF_D), BF16),
        compiler_params=pltpu.CompilerParams(vmem_limit_bytes=VMEM),
        name="rows",
    )(at, *parts)


def add_over_slice(stats):
    for axis in (LINE, "y", "z"):
        spread = jnp.broadcast_to(stats[None], (lax.axis_size(axis), *stats.shape))
        stats = jnp.sum(lax.all_to_all(spread, axis, 0, 0, tiled=True), axis=0)
    return stats


def pick_rows(block, count, core):
    out = lax.broadcasted_iota(jnp.int32, (count, 2 * count), 0)
    src = lax.broadcasted_iota(jnp.int32, (count, 2 * count), 1)
    pick = (src == out // 6 * 12 + core * 6 + out % 6).astype(BF16)
    return jnp.dot(pick, block, preferred_element_type=F32).astype(BF16)


def shards(hidden, head, targets, loss_mask):
    rep, tok, y, z, core = (lax.axis_index(a) for a in ("rep", "tok", "y", "z", "core"))
    x = tok * 2 + rep
    states = hidden[0]

    sync = lax.optimization_barrier

    slab = pick_rows(lax.dynamic_slice(states, (z * 48, y * 896), (48, 896)), 24, core)
    piece = jnp.concatenate([line_xor(slab, 2), line_xor(slab, 3)], axis=0)[None]
    piece = jnp.concatenate([piece] + [axis_xor(piece, "y", k) for k in (1, 2, 3)])
    piece, head, states = sync((piece, head, states))
    far = lax.all_gather(piece[None], "z", axis=0, tiled=True)

    got = []
    for n in range(2):
        sent = lax.dynamic_slice(head, (n * 896, (3 - x) * QUARTER), (896, QUARTER))
        got.append(line_xor(sent, 3))
    own = pick_rows(states, ROWS, core)
    nbr = [line_xor(own[:96], 1)]
    mate = axis_xor(lax.dynamic_slice(head, (0, x * QUARTER), (HALF_D, QUARTER)), "core", 1)

    voc = (y * 8 + z) * 2
    begin = [(voc + c) * 2048 + x * QUARTER for c in (core, 1 - core)]
    at = jnp.stack([tok, x, y, z, begin[0], begin[1]]).astype(jnp.int32)
    scal = jnp.stack([targets, loss_mask]).reshape(2, 32, 2, 6)
    scal = lax.dynamic_index_in_dim(scal, core, 2, keepdims=False).reshape(2, ROWS)
    scal = jnp.stack([scal, line_xor(scal, 2)], axis=1)
    mask = scal[1].astype(F32)
    tgt_wide = jnp.broadcast_to(scal[0][..., None], (2, ROWS, 128))
    mask_wide = jnp.broadcast_to(mask[..., None], (2, ROWS, 128))

    head, tgt_wide, mask_wide, mate, got[0], nbr[0], own = sync(
        (head, tgt_wide, mask_wide, mate, got[0], nbr[0], own)
    )
    nbr.append(line_xor(own[96:], 1))
    got_mate = [axis_xor(got[0], "core", 1)]
    head_t = head.T
    head_t, got[1], got_mate[0] = sync((head_t, got[1], got_mate[0]))
    got_mate.append(axis_xor(got[1], "core", 1))
    got = got + got_mate

    logits, stats = logits_call(at, own, nbr, far, head, mate, got, tgt_wide)
    head_t, stats = sync((head_t, stats))
    mate_t = axis_xor(head_t, "core", 1)
    stats = add_over_slice(stats)

    mine, theirs = grad_call(at, logits, stats, tgt_wide, mask_wide)
    grads = [mine, line_xor(theirs, 1), line_xor(mine, 2), line_xor(theirs, 3)]
    terms = terms_call(at, grads[:1], head_t, mate_t, (0,))
    terms = terms_call(at, grads[1:2], head_t, mate_t, (1,), terms)
    parts = list(terms_call(at, grads[2:], head_t, mate_t, (2, 3), terms, last=True))

    stats, parts[0] = sync((stats, parts[0]))
    stats = lax.dynamic_index_in_dim(stats, x, 0, keepdims=False)
    own_total, partner_total, picked, cross = (stats[s, :ROWS] for s in range(4))
    own_lse, partner_lse = jnp.log(own_total), jnp.log(partner_total)
    loss = mask[0] * (
        own_lse - picked + kl_weight * (cross / partner_total - partner_lse + own_lse)
    )
    pair = jnp.stack([loss, axis_xor(loss, "core", 1)]).reshape(2, 32, 6)
    pair = jnp.where(core == 0, pair, pair[::-1])
    token_loss = pair.transpose(1, 0, 2).reshape(1, 384)

    parts = [parts[0]] + [axis_xor(parts[k], "y", k) for k in (1, 2, 3)]
    token_loss, parts[0] = sync((token_loss, parts[0]))
    low = lax.all_to_all(rows_call(at, parts), ("tok", "z"), 0, 0, tiled=True)
    total = jnp.sum(low.reshape(2, 8, 8, HALF_D).astype(F32), axis=1)[:, :6]
    out = jnp.concatenate([total[0], total[1]], axis=1)
    return out.astype(BF16)[None], token_loss


def solution(mesh):
    fine = Mesh(
        mesh.devices.reshape(2, 2, N_Y, N_Z, N_C), ("rep", "tok", "y", "z", "core")
    )
    voc = ("y", "z", "core")
    placed = (P("rep", "tok", None), P("tok", voc), P("tok"), P("tok"))
    return jax.shard_map(
        shards,
        mesh=fine,
        in_specs=placed,
        out_specs=(P("rep", ("tok", *voc), None), P("rep", "tok")),
        check_vma=False,
    )
```

```python
import functools

import jax
import jax.numpy as jnp
from jax import lax
from jax.experimental import pallas as pl
from jax.experimental.pallas import tpu as pltpu
from jax.sharding import Mesh, PartitionSpec as P

softcap_limit = 30.0
kl_weight = 0.5
loss_scale = 16.0

N_Y, N_Z, N_C, N_X = 4, 8, 2, 4
LINE = ("rep", "tok")
ROWS = 192
QUARTER = 512
HALF_D = 1792
CHUNKS = (1344, 448)
TILE = 256
WIDE = 896
VMEM = 50 * 1024 * 1024
F32, BF16 = jnp.float32, jnp.bfloat16


def line_xor(block, k):
    k = (k % 2) * 2 + k // 2
    return lax.ppermute(block, LINE, [(x, x ^ k) for x in range(N_X)])


def axis_xor(block, axis, k):
    return lax.ppermute(block, axis, [(i, i ^ k) for i in range(lax.axis_size(axis))])


def whole(*shape):
    return pl.BlockSpec(shape, lambda s, at: (0,) * len(shape))


def logits_kernel(at, own, nbr, *refs):
    far, head, mate, got, tgt = refs[0], refs[1], refs[2], refs[3:7], refs[7]
    logits, stats, rows, raw, sums = refs[8:]
    step = pl.program_id(0)
    tok, y = at[0], at[2]

    @pl.when(step == 0)
    def _():
        for side in range(2):
            half = tok if side == 0 else 1 - tok
            begin = pl.multiple_of(half * HALF_D, 128)
            to = pl.ds(side * HALF_D, HALF_D)
            rows[0:ROWS, to] = own[:, pl.ds(begin, HALF_D)]
            rows[ROWS : 2 * ROWS, to] = nbr[:, pl.ds(begin, HALF_D)]
        for k in range(4):
            d = y ^ k
            column = pl.multiple_of((d // 2 ^ tok) * HALF_D + d % 2 * 896, 128)
            rows[2 * ROWS :, pl.ds(column, 896)] = far[:, k].reshape(2 * ROWS, 896)
        sums[...] = jnp.zeros_like(sums)

    lane = lax.broadcasted_iota(jnp.int32, (48, TILE), 1)

    def one(head, got, part, core):
        weights = jnp.concatenate([head[...]] + [chunk[...] for chunk in got], axis=0)
        raw[...] = jnp.dot(rows[...], weights, preferred_element_type=F32)
        column = lane + (at[4 + core] + part * TILE)
        for chunk in range(8):
            pair, g = chunk // 4, chunk % 4
            here = slice(g * 48, g * 48 + 48)
            if pair == 0:
                both = [raw[here], raw[ROWS + g * 48 : ROWS + g * 48 + 48]]
            else:
                begin = 2 * ROWS + g * 96
                pieces = [raw[begin + 24 * i : begin + 24 * i + 24] for i in range(4)]
                both = [jnp.concatenate(pieces[i::2], axis=0) for i in range(2)]
            both = [softcap_limit * jnp.tanh(v * (1.0 / softcap_limit)) for v in both]
            target = tgt[pair, here]
            hit = column == jnp.concatenate([target, target], axis=1)
            shared = [v.astype(BF16).astype(F32) for v in both]
            partner = [jnp.exp(v) for v in shared]
            for i in range(2):
                j = pair * 2 + i
                mine = both[i]
                logits[j, here] = mine
                terms = (
                    jnp.exp(mine),
                    partner[1 - i],
                    jnp.where(hit, mine, 0.0),
                    partner[1 - i] * (shared[1 - i] - mine),
                )
                for s, term in enumerate(terms):
                    sums[s, j, here] += term[:, :128] + term[:, 128:]

    for part in range(2):
        for core in range(2):
            @pl.when(step == part * 2 + core)
            def _(part=part, core=core):
                one((head, mate)[core], got[core * 2 : core * 2 + 2], part, core)

    @pl.when(step == 3)
    def _():
        lane = lax.broadcasted_iota(jnp.int32, (ROWS, 128), 1)
        stats[...] = jnp.zeros_like(stats)
        for j in range(4):
            wide = jnp.zeros((ROWS, 128), F32)
            for s in range(4):
                at_lane = (at[1] ^ j) % 2 * 4 + s
                wide = jnp.where(lane == at_lane, jnp.sum(sums[s, j], axis=1, keepdims=True), wide)
            wide = jnp.concatenate([wide, jnp.zeros((256 - ROWS, 128), F32)], axis=0)
            stats[(at[1] ^ j) // 2] += wide.T[:8]


def logits_call(at, own, nbr, far, head, mate, got, tgt):
    weights = pl.BlockSpec((HALF_D, TILE), lambda s, at: (0, at[1] * 2 + s // 2))
    return pl.pallas_call(
        logits_kernel,
        grid_spec=pltpu.PrefetchScalarGridSpec(
            num_scalar_prefetch=1,
            grid=(4,),
            in_specs=[whole(ROWS, 2 * HALF_D)] * 2
            + [whole(8, 4, 48, 896)]
            + [weights, pl.BlockSpec((HALF_D, TILE), lambda s, at: (0, s // 2))]
            + [pl.BlockSpec((c, TILE), lambda s, at: (0, s // 2)) for c in CHUNKS] * 2
            + [whole(2, ROWS, 128)],
            out_specs=[
                pl.BlockSpec((4, ROWS, TILE), lambda s, at: (0, 0, s % 2 * 2 + s // 2)),
                whole(2, 8, 256),
            ],
            scratch_shapes=[
                pltpu.VMEM((4 * ROWS, 2 * HALF_D), BF16),
                pltpu.VMEM((4 * ROWS, TILE), F32),
                pltpu.VMEM((4, 4, ROWS, 128), F32),
            ],
        ),
        out_shape=[
            jax.ShapeDtypeStruct((4, ROWS, 4 * TILE), F32),
            jax.ShapeDtypeStruct((2, 8, 256), F32),
        ],
        compiler_params=pltpu.CompilerParams(vmem_limit_bytes=VMEM),
        cost_estimate=pl.CostEstimate(
            flops=4 * ROWS * 4 * TILE * 2 * HALF_D * 2, bytes_accessed=16 << 20, transcendentals=1 << 21
        ),
        name="logits",
    )(at, own, nbr, far, head, mate, *got, tgt)


def grad_kernel(at, logits, stats, tgt, mask, mine, theirs, scales):
    step = pl.program_id(0)

    @pl.when(step == 0)
    def _():
        for j in range(4):
            block = at[1] ^ j
            total = stats[block // 2].T[:ROWS]
            total = jnp.where(block % 2 == 0, total[:, 0:2], total[:, 4:6])
            weight = loss_scale * mask[j // 2]
            scales[0, j] = (1.0 + kl_weight) * weight / total[:, 0:1]
            scales[1, j] = kl_weight * weight / total[:, 1:2]

    core, part = step // 2, step % 2
    column = lax.broadcasted_iota(jnp.int32, (48, TILE), 1)
    column = column + (jnp.where(core == 0, at[4], at[5]) + part * TILE)

    for pair in range(2):
        for g in range(4):
            here = slice(g * 48, g * 48 + 48)
            both = [logits[pair * 2, here], logits[pair * 2 + 1, here]]
            target, weight = tgt[pair, here], loss_scale * mask[pair, here]
            target = jnp.concatenate([target, target], axis=1)
            weight = jnp.concatenate([weight, weight], axis=1)
            hit = jnp.where(column == target, weight, 0.0)
            for i in range(2):
                own = both[i]
                shared = both[1 - i].astype(BF16).astype(F32)
                own_scale, partner_scale = (
                    jnp.concatenate([scales[n, pair * 2 + i, here]] * 2, axis=1) for n in range(2)
                )
                slope = own * (1.0 / softcap_limit)
                value = jnp.exp(own) * own_scale - hit - jnp.exp(shared) * partner_scale
                (mine, theirs)[i][pair, here] = (value * (1.0 - slope * slope)).astype(BF16)


def grad_call(at, logits, stats, tgt, mask):
    out = pl.BlockSpec((2, ROWS, TILE), lambda s, at: (0, 0, s))
    return pl.pallas_call(
        grad_kernel,
        grid_spec=pltpu.PrefetchScalarGridSpec(
            num_scalar_prefetch=1,
            grid=(4,),
            in_specs=[
                pl.BlockSpec((4, ROWS, TILE), lambda s, at: (0, 0, s)),
                whole(2, 8, 256),
                whole(2, ROWS, 128),
                whole(2, ROWS, 128),
            ],
            out_specs=[out, out],
            scratch_shapes=[pltpu.VMEM((2, 4, ROWS, 128), F32)],
        ),
        out_shape=[jax.ShapeDtypeStruct((2, ROWS, 4 * TILE), BF16)] * 2,
        compiler_params=pltpu.CompilerParams(vmem_limit_bytes=VMEM // 3),
        name="logit_grad",
    )(at, logits, stats, tgt, mask)


def terms_kernel(at, *refs, ks, add, last):
    refs = list(refs)
    left, right = [], []
    for k in ks:
        grad, head, mate = refs[:3]
        refs = refs[3:]
        order = (0, 1) if k < 2 else (1, 0)
        left.append(jnp.concatenate([grad[t] for t in order], axis=0))
        right += [head[...], mate[...]]
    total = jnp.dot(
        jnp.concatenate(left, axis=1),
        jnp.concatenate(right, axis=0),
        preferred_element_type=F32,
    )
    if add:
        total = total + refs.pop(0)[...]
    if not last:
        refs[0][...] = total
        return
    outs, scratch = refs[:4], refs[4]
    for tok in range(2):
        for y in range(4):
            begin = tok * ROWS + y * 48
            scratch[y, tok] = total[begin : begin + 48]
    for k in range(4):
        outs[k][...] = scratch[at[2] ^ k].astype(outs[k].dtype)


def terms_call(at, grads, head, mate, ks, acc=None, last=False):
    tile = pl.BlockSpec((2 * ROWS, WIDE), lambda s, at: (0, s))
    in_specs, args = [], []
    for k, grad in zip(ks, grads):
        weights = pl.BlockSpec((QUARTER, WIDE), lambda s, at, k=k: (at[1] ^ k, s))
        in_specs += [pl.BlockSpec((2, ROWS, 4 * TILE), lambda s, at: (0, 0, 0)), weights, weights]
        args += [grad, head, mate]
    out_specs, scratch = tile, []
    out_shape = jax.ShapeDtypeStruct((2 * ROWS, HALF_D), F32)
    if acc is not None:
        in_specs.append(tile)
        args.append(acc)
    if last:
        out_specs = [pl.BlockSpec((2, 48, WIDE), lambda s, at: (0, 0, s))] * 4
        out_shape = [jax.ShapeDtypeStruct((2, 48, HALF_D), t) for t in (F32, BF16, BF16, BF16)]
        scratch = [pltpu.VMEM((4, 2, 48, WIDE), F32)]
    return pl.pallas_call(
        functools.partial(terms_kernel, ks=ks, add=acc is not None, last=last),
        grid_spec=pltpu.PrefetchScalarGridSpec(
            num_scalar_prefetch=1,
            grid=(HALF_D // WIDE,),
            in_specs=in_specs,
            out_specs=out_specs,
            scratch_shapes=scratch,
        ),
        out_shape=out_shape,
        compiler_params=pltpu.CompilerParams(vmem_limit_bytes=VMEM * 3 // 5),
        cost_estimate=pl.CostEstimate(
            flops=2 * 2 * ROWS * HALF_D * 2 * QUARTER * len(ks),
            bytes_accessed=(6 << 20) * len(ks),
            transcendentals=0,
        ),
        name="gradient_terms",
    )(at, *args)


def rows_kernel(at, *refs):
    parts, out_ref = refs[:4], refs[4]
    total = parts[0][...]
    for part in parts[1:]:
        total = total + part[...].astype(F32)
    out = lax.broadcasted_iota(jnp.int32, (128, 96), 0)
    src = lax.broadcasted_iota(jnp.int32, (128, 96), 1)
    i = out & 7
    wanted = ((out >> 6) ^ at[0]) * 48 + ((out >> 3) & 7) * 6 + i
    pick = jnp.where((src == wanted) & (i < 6), 1.0, 0.0).astype(BF16)
    low = jnp.dot(pick, total.reshape(96, 896).astype(BF16), preferred_element_type=F32)
    out_ref[...] = low.reshape(16, 8, 896).astype(BF16)


def rows_call(at, parts):
    return pl.pallas_call(
        rows_kernel,
        grid_spec=pltpu.PrefetchScalarGridSpec(
            num_scalar_prefetch=1,
            grid=(2,),
            in_specs=[pl.BlockSpec((2, 48, 896), lambda s, at: (0, 0, s))] * 4,
            out_specs=pl.BlockSpec((16, 8, 896), lambda s, at: (0, 0, s)),
        ),
        out_shape=jax.ShapeDtypeStruct((16, 8, HALF_D), BF16),
        compiler_params=pltpu.CompilerParams(vmem_limit_bytes=VMEM // 3),
        name="rows",
    )(at, *parts)


def add_over_slice(stats):
    for axis in (LINE, "y", "z"):
        spread = jnp.broadcast_to(stats[None], (lax.axis_size(axis), *stats.shape))
        stats = jnp.sum(lax.all_to_all(spread, axis, 0, 0, tiled=True), axis=0)
    return stats


def pick_rows(block, count, core):
    out = lax.broadcasted_iota(jnp.int32, (count, 2 * count), 0)
    src = lax.broadcasted_iota(jnp.int32, (count, 2 * count), 1)
    pick = (src == out // 6 * 12 + core * 6 + out % 6).astype(BF16)
    return jnp.dot(pick, block, preferred_element_type=F32).astype(BF16)


def shards(hidden, head, targets, loss_mask):
    rep, tok, y, z, core = (lax.axis_index(a) for a in ("rep", "tok", "y", "z", "core"))
    x = tok * 2 + rep
    states = hidden[0]

    sync = lax.optimization_barrier

    scal = jnp.stack([targets, loss_mask]).reshape(2, 32, 2, 6)
    scal = lax.dynamic_index_in_dim(scal, core, 2, keepdims=False).reshape(2, ROWS)
    slab = pick_rows(lax.dynamic_slice(states, (z * 48, y * 896), (48, 896)), 24, core)
    piece = jnp.concatenate([line_xor(slab, 2), line_xor(slab, 3)], axis=0)[None]
    far_scal = line_xor(scal, 2)
    sent = [
        lax.dynamic_slice(head, (n * CHUNKS[0], (3 - x) * QUARTER), (CHUNKS[n], QUARTER))
        for n in range(2)
    ]
    piece, far_scal, sent[0] = sync((piece, far_scal, sent[0]))
    got = [line_xor(sent[0], 3)]
    piece = jnp.concatenate([piece] + [axis_xor(piece, "y", k) for k in (1, 2, 3)])
    own = pick_rows(states, ROWS, core)
    piece, own = sync((piece, own))
    far = lax.all_gather(piece[None], "z", axis=0, tiled=True)
    nbr = line_xor(own, 1)
    mate = axis_xor(lax.dynamic_slice(head, (0, x * QUARTER), (HALF_D, QUARTER)), "core", 1)

    voc = (y * 8 + z) * 2
    begin = [(voc + c) * 2048 + x * QUARTER for c in (core, 1 - core)]
    at = jnp.stack([tok, x, y, z, begin[0], begin[1]]).astype(jnp.int32)
    scal = jnp.stack([scal, far_scal], axis=1)
    mask = scal[1].astype(F32)
    tgt_wide = jnp.broadcast_to(scal[0][..., None], (2, ROWS, 128))
    mask_wide = jnp.broadcast_to(mask[..., None], (2, ROWS, 128))

    head_t = head.T
    head_t, tgt_wide, mask_wide, mate, got[0], nbr, sent[1] = sync(
        (head_t, tgt_wide, mask_wide, mate, got[0], nbr, sent[1])
    )
    got.append(line_xor(sent[1], 3))
    got_mate = [axis_xor(g, "core", 1) for g in got]
    got = got + got_mate

    logits, stats = logits_call(at, own, nbr, far, head, mate, got, tgt_wide)
    head_t, stats = sync((head_t, stats))
    mate_t = axis_xor(head_t, "core", 1)
    stats = add_over_slice(stats)

    mine, theirs = grad_call(at, logits, stats, tgt_wide, mask_wide)
    grads = [mine, line_xor(theirs, 1), line_xor(mine, 2), line_xor(theirs, 3)]
    terms = terms_call(at, grads[:1], head_t, mate_t, (0,))
    terms = terms_call(at, grads[1:2], head_t, mate_t, (1,), terms)
    parts = list(terms_call(at, grads[2:], head_t, mate_t, (2, 3), terms, last=True))

    stats, parts[0] = sync((stats, parts[0]))
    stats = lax.dynamic_index_in_dim(stats.reshape(4, 4, 256), x, 0, keepdims=False)
    own_total, partner_total, picked, cross = (stats[s, :ROWS] for s in range(4))
    own_lse, partner_lse = jnp.log(own_total), jnp.log(partner_total)
    loss = mask[0] * (
        own_lse - picked + kl_weight * (cross / partner_total - partner_lse + own_lse)
    )
    pair = jnp.stack([loss, axis_xor(loss, "core", 1)]).reshape(2, 32, 6)
    pair = jnp.where(core == 0, pair, pair[::-1])
    token_loss = pair.transpose(1, 0, 2).reshape(1, 384)

    parts = [parts[0]] + [axis_xor(parts[k], "y", k) for k in (1, 2, 3)]
    token_loss, parts[0] = sync((token_loss, parts[0]))
    low = lax.all_to_all(rows_call(at, parts), ("tok", "z"), 0, 0, tiled=True)
    total = jnp.sum(low.reshape(2, 8, 8, HALF_D).astype(F32), axis=1)[:, :6]
    out = jnp.concatenate([total[0], total[1]], axis=1)
    return out.astype(BF16)[None], token_loss


def solution(mesh):
    fine = Mesh(
        mesh.devices.reshape(2, 2, N_Y, N_Z, N_C), ("rep", "tok", "y", "z", "core")
    )
    voc = ("y", "z", "core")
    placed = (P("rep", "tok", None), P("tok", voc), P("tok"), P("tok"))
    return jax.shard_map(
        shards,
        mesh=fine,
        in_specs=placed,
        out_specs=(P("rep", ("tok", *voc), None), P("rep", "tok")),
        check_vma=False,
    )
```

```python
import functools

import jax
import jax.numpy as jnp
from jax import lax
from jax.experimental import pallas as pl
from jax.experimental.pallas import tpu as pltpu
from jax.sharding import Mesh, PartitionSpec as P

softcap_limit = 30.0
kl_weight = 0.5
loss_scale = 16.0

N_Y, N_Z, N_C, N_X = 4, 8, 2, 4
LINE = ("rep", "tok")
ROWS = 192
QUARTER = 512
HALF_D = 1792
CHUNKS = (1344, 448)
TILE = 256
WIDE = 896
VMEM = 50 * 1024 * 1024
F32, BF16 = jnp.float32, jnp.bfloat16


def line_xor(block, k):
    k = (k % 2) * 2 + k // 2
    return lax.ppermute(block, LINE, [(x, x ^ k) for x in range(N_X)])


def axis_xor(block, axis, k):
    return lax.ppermute(block, axis, [(i, i ^ k) for i in range(lax.axis_size(axis))])


def whole(*shape):
    return pl.BlockSpec(shape, lambda s, at: (0,) * len(shape))


def logits_kernel(at, own, nbr, *refs):
    far, head, mate, got, tgt = refs[0], refs[1], refs[2], refs[3:7], refs[7]
    logits, stats, rows, raws, sums = refs[8], refs[9], refs[10], refs[11:13], refs[13]
    step = pl.program_id(0)
    tok, y = at[0], at[2]

    @pl.when(step == 0)
    def _():
        for side in range(2):
            half = tok if side == 0 else 1 - tok
            begin = pl.multiple_of(half * HALF_D, 128)
            to = pl.ds(side * HALF_D, HALF_D)
            rows[0:ROWS, to] = own[:, pl.ds(begin, HALF_D)]
            rows[ROWS : 2 * ROWS, to] = nbr[:, pl.ds(begin, HALF_D)]
        for k in range(4):
            d = y ^ k
            column = pl.multiple_of((d // 2 ^ tok) * HALF_D + d % 2 * 896, 128)
            rows[2 * ROWS :, pl.ds(column, 896)] = far[:, k].reshape(2 * ROWS, 896)
        sums[...] = jnp.zeros_like(sums)

    lane = lax.broadcasted_iota(jnp.int32, (48, TILE), 1)

    def product(raw, head, got):
        weights = jnp.concatenate([head[...]] + [chunk[...] for chunk in got], axis=0)
        raw[...] = jnp.dot(rows[...], weights, preferred_element_type=F32)

    def work(raw, part, core):
        column = lane + (at[4 + core] + part * TILE)
        for chunk in range(8):
            pair, g = chunk // 4, chunk % 4
            here = slice(g * 48, g * 48 + 48)
            if pair == 0:
                both = [raw[here], raw[ROWS + g * 48 : ROWS + g * 48 + 48]]
            else:
                begin = 2 * ROWS + g * 96
                pieces = [raw[begin + 24 * i : begin + 24 * i + 24] for i in range(4)]
                both = [jnp.concatenate(pieces[i::2], axis=0) for i in range(2)]
            both = [softcap_limit * jnp.tanh(v * (1.0 / softcap_limit)) for v in both]
            target = tgt[pair, here]
            hit = column == jnp.concatenate([target, target], axis=1)
            shared = [v.astype(BF16).astype(F32) for v in both]
            partner = [jnp.exp(v) for v in shared]
            for i in range(2):
                j = pair * 2 + i
                mine = both[i]
                logits[j, here] = mine
                terms = (
                    jnp.exp(mine),
                    partner[1 - i],
                    jnp.where(hit, mine, 0.0),
                    partner[1 - i] * (shared[1 - i] - mine),
                )
                for s, term in enumerate(terms):
                    sums[s, j, here] += term[:, :128] + term[:, 128:]

    for n in range(5):
        @pl.when(step == n)
        def _(n=n):
            if n < 4:
                core = n % 2
                product(raws[n % 2], (head, mate)[core], got[core * 2 : core * 2 + 2])
            if n > 0:
                work(raws[(n - 1) % 2], (n - 1) // 2, (n - 1) % 2)

    @pl.when(step == 4)
    def _():
        lane = lax.broadcasted_iota(jnp.int32, (ROWS, 128), 1)
        stats[...] = jnp.zeros_like(stats)
        for j in range(4):
            wide = jnp.zeros((ROWS, 128), F32)
            for s in range(4):
                at_lane = (at[1] ^ j) % 2 * 4 + s
                wide = jnp.where(lane == at_lane, jnp.sum(sums[s, j], axis=1, keepdims=True), wide)
            wide = jnp.concatenate([wide, jnp.zeros((256 - ROWS, 128), F32)], axis=0)
            stats[(at[1] ^ j) // 2] += wide.T[:8]


def logits_call(at, own, nbr, far, head, mate, got, tgt):
    def once(*shape):
        return pl.BlockSpec(
            shape, lambda s, at: (0,) * len(shape), pipeline_mode=pl.Buffered(1)
        )

    def part(s):
        return jnp.minimum(s // 2, 1)

    def tile(s, at):
        done = jnp.maximum(s - 1, 0)
        return (0, 0, done % 2 * 2 + done // 2)

    return pl.pallas_call(
        logits_kernel,
        grid_spec=pltpu.PrefetchScalarGridSpec(
            num_scalar_prefetch=1,
            grid=(5,),
            in_specs=[once(ROWS, 2 * HALF_D)] * 2
            + [once(8, 4, 48, 896)]
            + [
                pl.BlockSpec((HALF_D, TILE), lambda s, at: (0, at[1] * 2 + part(s))),
                pl.BlockSpec((HALF_D, TILE), lambda s, at: (0, part(s))),
            ]
            + [pl.BlockSpec((c, TILE), lambda s, at: (0, part(s))) for c in CHUNKS] * 2
            + [whole(2, ROWS, 128)],
            out_specs=[pl.BlockSpec((4, ROWS, TILE), tile), whole(2, 8, 256)],
            scratch_shapes=[
                pltpu.VMEM((4 * ROWS, 2 * HALF_D), BF16),
                pltpu.VMEM((4 * ROWS, TILE), F32),
                pltpu.VMEM((4 * ROWS, TILE), F32),
                pltpu.VMEM((4, 4, ROWS, 128), F32),
            ],
        ),
        out_shape=[
            jax.ShapeDtypeStruct((4, ROWS, 4 * TILE), F32),
            jax.ShapeDtypeStruct((2, 8, 256), F32),
        ],
        compiler_params=pltpu.CompilerParams(vmem_limit_bytes=VMEM),
        cost_estimate=pl.CostEstimate(
            flops=4 * ROWS * 4 * TILE * 2 * HALF_D * 2, bytes_accessed=16 << 20, transcendentals=1 << 21
        ),
        name="logits",
    )(at, own, nbr, far, head, mate, *got, tgt)


def grad_kernel(at, logits, stats, tgt, mask, mine, theirs, scales):
    step = pl.program_id(0)

    @pl.when(step == 0)
    def _():
        for j in range(4):
            block = at[1] ^ j
            total = stats[block // 2].T[:ROWS]
            total = jnp.where(block % 2 == 0, total[:, 0:2], total[:, 4:6])
            weight = loss_scale * mask[j // 2]
            scales[0, j] = (1.0 + kl_weight) * weight / total[:, 0:1]
            scales[1, j] = kl_weight * weight / total[:, 1:2]

    core, part = step // 2, step % 2
    column = lax.broadcasted_iota(jnp.int32, (48, TILE), 1)
    column = column + (jnp.where(core == 0, at[4], at[5]) + part * TILE)

    for pair in range(2):
        for g in range(4):
            here = slice(g * 48, g * 48 + 48)
            both = [logits[pair * 2, here], logits[pair * 2 + 1, here]]
            target, weight = tgt[pair, here], loss_scale * mask[pair, here]
            target = jnp.concatenate([target, target], axis=1)
            weight = jnp.concatenate([weight, weight], axis=1)
            hit = jnp.where(column == target, weight, 0.0)
            for i in range(2):
                own = both[i]
                shared = both[1 - i].astype(BF16).astype(F32)
                own_scale, partner_scale = (
                    jnp.concatenate([scales[n, pair * 2 + i, here]] * 2, axis=1) for n in range(2)
                )
                slope = own * (1.0 / softcap_limit)
                value = jnp.exp(own) * own_scale - hit - jnp.exp(shared) * partner_scale
                (mine, theirs)[i][pair, here] = (value * (1.0 - slope * slope)).astype(BF16)


def grad_call(at, logits, stats, tgt, mask):
    out = pl.BlockSpec((2, ROWS, TILE), lambda s, at: (0, 0, s))
    return pl.pallas_call(
        grad_kernel,
        grid_spec=pltpu.PrefetchScalarGridSpec(
            num_scalar_prefetch=1,
            grid=(4,),
            in_specs=[
                pl.BlockSpec((4, ROWS, TILE), lambda s, at: (0, 0, s)),
                whole(2, 8, 256),
                whole(2, ROWS, 128),
                whole(2, ROWS, 128),
            ],
            out_specs=[out, out],
            scratch_shapes=[pltpu.VMEM((2, 4, ROWS, 128), F32)],
        ),
        out_shape=[jax.ShapeDtypeStruct((2, ROWS, 4 * TILE), BF16)] * 2,
        compiler_params=pltpu.CompilerParams(vmem_limit_bytes=VMEM),
        name="logit_grad",
    )(at, logits, stats, tgt, mask)


def terms_kernel(at, *refs, ks, add, last):
    refs = list(refs)
    left, right = [], []
    for k in ks:
        grad, head, mate = refs[:3]
        refs = refs[3:]
        order = (0, 1) if k < 2 else (1, 0)
        left.append(jnp.concatenate([grad[t] for t in order], axis=0))
        right += [head[...], mate[...]]
    total = jnp.dot(
        jnp.concatenate(left, axis=1),
        jnp.concatenate(right, axis=0),
        preferred_element_type=F32,
    )
    if add:
        total = total + refs.pop(0)[...]
    if not last:
        refs[0][...] = total
        return
    outs, scratch = refs[:4], refs[4]
    for tok in range(2):
        for y in range(4):
            begin = tok * ROWS + y * 48
            scratch[y, tok] = total[begin : begin + 48]
    for k in range(4):
        outs[k][...] = scratch[at[2] ^ k].astype(outs[k].dtype)


def terms_call(at, grads, head, mate, ks, acc=None, last=False):
    tile = pl.BlockSpec((2 * ROWS, WIDE), lambda s, at: (0, s))
    in_specs, args = [], []
    for k, grad in zip(ks, grads):
        weights = pl.BlockSpec((QUARTER, WIDE), lambda s, at, k=k: (at[1] ^ k, s))
        in_specs += [pl.BlockSpec((2, ROWS, 4 * TILE), lambda s, at: (0, 0, 0)), weights, weights]
        args += [grad, head, mate]
    out_specs, scratch = tile, []
    out_shape = jax.ShapeDtypeStruct((2 * ROWS, HALF_D), F32)
    if acc is not None:
        in_specs.append(tile)
        args.append(acc)
    if last:
        out_specs = [pl.BlockSpec((2, 48, WIDE), lambda s, at: (0, 0, s))] * 4
        out_shape = [jax.ShapeDtypeStruct((2, 48, HALF_D), t) for t in (F32, BF16, BF16, BF16)]
        scratch = [pltpu.VMEM((4, 2, 48, WIDE), F32)]
    return pl.pallas_call(
        functools.partial(terms_kernel, ks=ks, add=acc is not None, last=last),
        grid_spec=pltpu.PrefetchScalarGridSpec(
            num_scalar_prefetch=1,
            grid=(HALF_D // WIDE,),
            in_specs=in_specs,
            out_specs=out_specs,
            scratch_shapes=scratch,
        ),
        out_shape=out_shape,
        compiler_params=pltpu.CompilerParams(vmem_limit_bytes=VMEM * 3 // 5),
        cost_estimate=pl.CostEstimate(
            flops=2 * 2 * ROWS * HALF_D * 2 * QUARTER * len(ks),
            bytes_accessed=(6 << 20) * len(ks),
            transcendentals=0,
        ),
        name="gradient_terms",
    )(at, *args)


def rows_kernel(at, *refs):
    parts, out_ref = refs[:4], refs[4]
    total = parts[0][...]
    for part in parts[1:]:
        total = total + part[...].astype(F32)
    out = lax.broadcasted_iota(jnp.int32, (128, 96), 0)
    src = lax.broadcasted_iota(jnp.int32, (128, 96), 1)
    i = out & 7
    wanted = ((out >> 6) ^ at[0]) * 48 + ((out >> 3) & 7) * 6 + i
    pick = jnp.where((src == wanted) & (i < 6), 1.0, 0.0).astype(BF16)
    low = jnp.dot(pick, total.reshape(96, 896).astype(BF16), preferred_element_type=F32)
    out_ref[...] = low.reshape(16, 8, 896).astype(BF16)


def rows_call(at, parts):
    return pl.pallas_call(
        rows_kernel,
        grid_spec=pltpu.PrefetchScalarGridSpec(
            num_scalar_prefetch=1,
            grid=(2,),
            in_specs=[pl.BlockSpec((2, 48, 896), lambda s, at: (0, 0, s))] * 4,
            out_specs=pl.BlockSpec((16, 8, 896), lambda s, at: (0, 0, s)),
        ),
        out_shape=jax.ShapeDtypeStruct((16, 8, HALF_D), BF16),
        compiler_params=pltpu.CompilerParams(vmem_limit_bytes=VMEM // 3),
        name="rows",
    )(at, *parts)


def add_over_slice(stats):
    for axis in ((*LINE, "y"), "z"):
        spread = jnp.broadcast_to(stats[None], (lax.axis_size(axis), *stats.shape))
        stats = jnp.sum(lax.all_to_all(spread, axis, 0, 0, tiled=True), axis=0)
    return stats


def pick_rows(block, count, core):
    out = lax.broadcasted_iota(jnp.int32, (count, 2 * count), 0)
    src = lax.broadcasted_iota(jnp.int32, (count, 2 * count), 1)
    pick = (src == out // 6 * 12 + core * 6 + out % 6).astype(BF16)
    return jnp.dot(pick, block, preferred_element_type=F32).astype(BF16)


def shards(hidden, head, targets, loss_mask):
    rep, tok, y, z, core = (lax.axis_index(a) for a in ("rep", "tok", "y", "z", "core"))
    x = tok * 2 + rep
    states = hidden[0]

    sync = lax.optimization_barrier

    scal = jnp.stack([targets, loss_mask]).reshape(2, 32, 2, 6)
    scal = lax.dynamic_index_in_dim(scal, core, 2, keepdims=False).reshape(2, ROWS)
    slab = pick_rows(lax.dynamic_slice(states, (z * 48, y * 896), (48, 896)), 24, core)
    piece = jnp.concatenate([line_xor(slab, 2), line_xor(slab, 3)], axis=0)[None]
    far_scal = line_xor(scal, 2)
    sent = [
        lax.dynamic_slice(head, (n * CHUNKS[0], (3 - x) * QUARTER), (CHUNKS[n], QUARTER))
        for n in range(2)
    ]
    piece, far_scal, *sent = sync((piece, far_scal, *sent))
    got = [line_xor(sent[0], 3)]
    piece = jnp.concatenate([piece] + [axis_xor(piece, "y", k) for k in (1, 2, 3)])
    own = pick_rows(states, ROWS, core)
    piece, own = sync((piece, own))
    far = lax.all_gather(piece[None], "z", axis=0, tiled=True)
    nbr = line_xor(own, 1)

    voc = (y * 8 + z) * 2
    begin = [(voc + c) * 2048 + x * QUARTER for c in (core, 1 - core)]
    at = jnp.stack([tok, x, y, z, begin[0], begin[1]]).astype(jnp.int32)
    scal = jnp.stack([scal, far_scal], axis=1)
    mask = scal[1].astype(F32)
    tgt_wide = jnp.broadcast_to(scal[0][..., None], (2, ROWS, 128))
    mask_wide = jnp.broadcast_to(mask[..., None], (2, ROWS, 128))

    head_t = head.T
    head_t, cut = sync((head_t, head))
    cut = lax.dynamic_slice(cut, (0, x * QUARTER), (HALF_D, QUARTER))
    head_t, tgt_wide, mask_wide, got[0], nbr, sent[1], cut = sync(
        (head_t, tgt_wide, mask_wide, got[0], nbr, sent[1], cut)
    )
    got.append(line_xor(sent[1], 3))
    mate = axis_xor(cut, "core", 1)
    got_mate = [axis_xor(g, "core", 1) for g in got]
    got = got + got_mate

    logits, stats = logits_call(at, own, nbr, far, head, mate, got, tgt_wide)
    head_t, stats = sync((head_t, stats))
    mate_t = axis_xor(head_t, "core", 1)
    stats = add_over_slice(stats)

    mine, theirs = grad_call(at, logits, stats, tgt_wide, mask_wide)
    grads = [mine, line_xor(theirs, 1), line_xor(mine, 2), line_xor(theirs, 3)]
    terms = terms_call(at, grads[:1], head_t, mate_t, (0,))
    terms = terms_call(at, grads[1:2], head_t, mate_t, (1,), terms)
    parts = list(terms_call(at, grads[2:], head_t, mate_t, (2, 3), terms, last=True))

    stats, parts[0] = sync((stats, parts[0]))
    stats = lax.dynamic_index_in_dim(stats.reshape(4, 4, 256), x, 0, keepdims=False)
    own_total, partner_total, picked, cross = (stats[s, :ROWS] for s in range(4))
    own_lse, partner_lse = jnp.log(own_total), jnp.log(partner_total)
    loss = mask[0] * (
        own_lse - picked + kl_weight * (cross / partner_total - partner_lse + own_lse)
    )
    pair = jnp.stack([loss, axis_xor(loss, "core", 1)]).reshape(2, 32, 6)
    pair = jnp.where(core == 0, pair, pair[::-1])
    token_loss = pair.transpose(1, 0, 2).reshape(1, 384)

    parts = [parts[0]] + [axis_xor(parts[k], "y", k) for k in (1, 2, 3)]
    token_loss, parts[0] = sync((token_loss, parts[0]))
    low = lax.all_to_all(rows_call(at, parts), ("tok", "z"), 0, 0, tiled=True)
    total = jnp.sum(low.reshape(2, 8, 8, HALF_D).astype(F32), axis=1)[:, :6]
    out = jnp.concatenate([total[0], total[1]], axis=1)
    return out.astype(BF16)[None], token_loss


def solution(mesh):
    fine = Mesh(
        mesh.devices.reshape(2, 2, N_Y, N_Z, N_C), ("rep", "tok", "y", "z", "core")
    )
    voc = ("y", "z", "core")
    placed = (P("rep", "tok", None), P("tok", voc), P("tok"), P("tok"))
    return jax.shard_map(
        shards,
        mesh=fine,
        in_specs=placed,
        out_specs=(P("rep", ("tok", *voc), None), P("rep", "tok")),
        check_vma=False,
    )
```

```python
import functools

import jax
import jax.numpy as jnp
from jax import lax
from jax.experimental import pallas as pl
from jax.experimental.pallas import tpu as pltpu
from jax.sharding import Mesh, PartitionSpec as P

softcap_limit = 30.0
kl_weight = 0.5
loss_scale = 16.0

N_Y, N_Z, N_C, N_X = 4, 8, 2, 4
LINE = ("rep", "tok")
ROWS = 192
QUARTER = 512
HALF_D = 1792
CHUNKS = (256, 1088, 448)
TILE = 256
WIDE = 896
VMEM = 50 * 1024 * 1024
F32, BF16 = jnp.float32, jnp.bfloat16


def line_xor(block, k):
    k = (k % 2) * 2 + k // 2
    return lax.ppermute(block, LINE, [(x, x ^ k) for x in range(N_X)])


def axis_xor(block, axis, k):
    return lax.ppermute(block, axis, [(i, i ^ k) for i in range(lax.axis_size(axis))])


def whole(*shape):
    return pl.BlockSpec(shape, lambda s, at: (0,) * len(shape))


def logits_kernel(at, own, nbr, *refs):
    far, head, mate, got, tgt = refs[0], refs[1], refs[2], refs[3:9], refs[9]
    logits, stats, rows, raws, sums = refs[10], refs[11], refs[12], refs[13:15], refs[15]
    step = pl.program_id(0)
    tok, y = at[0], at[2]

    @pl.when(step == 0)
    def _():
        for side in range(2):
            half = tok if side == 0 else 1 - tok
            begin = pl.multiple_of(half * HALF_D, 128)
            to = pl.ds(side * HALF_D, HALF_D)
            rows[0:ROWS, to] = own[:, pl.ds(begin, HALF_D)]
            rows[ROWS : 2 * ROWS, to] = nbr[:, pl.ds(begin, HALF_D)]
        for k in range(4):
            d = y ^ k
            column = pl.multiple_of((d // 2 ^ tok) * HALF_D + d % 2 * 896, 128)
            rows[2 * ROWS :, pl.ds(column, 896)] = far[:, k].reshape(2 * ROWS, 896)
        sums[...] = jnp.zeros_like(sums)

    lane = lax.broadcasted_iota(jnp.int32, (48, TILE), 1)

    def product(raw, head, got):
        weights = jnp.concatenate([head[...]] + [chunk[...] for chunk in got], axis=0)
        raw[...] = jnp.dot(rows[...], weights, preferred_element_type=F32)

    def work(raw, part, core):
        column = lane + (at[4 + core] + part * TILE)
        for chunk in range(8):
            pair, g = chunk // 4, chunk % 4
            here = slice(g * 48, g * 48 + 48)
            if pair == 0:
                both = [raw[here], raw[ROWS + g * 48 : ROWS + g * 48 + 48]]
            else:
                begin = 2 * ROWS + g * 96
                pieces = [raw[begin + 24 * i : begin + 24 * i + 24] for i in range(4)]
                both = [jnp.concatenate(pieces[i::2], axis=0) for i in range(2)]
            both = [softcap_limit * jnp.tanh(v * (1.0 / softcap_limit)) for v in both]
            target = tgt[pair, here]
            hit = column == jnp.concatenate([target, target], axis=1)
            shared = [v.astype(BF16).astype(F32) for v in both]
            partner = [jnp.exp(v) for v in shared]
            for i in range(2):
                j = pair * 2 + i
                mine = both[i]
                logits[j, here] = mine
                terms = (
                    jnp.exp(mine),
                    partner[1 - i],
                    jnp.where(hit, mine, 0.0),
                    partner[1 - i] * (shared[1 - i] - mine),
                )
                for s, term in enumerate(terms):
                    sums[s, j, here] += term[:, :128] + term[:, 128:]

    for n in range(5):
        @pl.when(step == n)
        def _(n=n):
            if n < 4:
                core = n % 2
                product(raws[n % 2], (head, mate)[core], got[core * 3 : core * 3 + 3])
            if n > 0:
                work(raws[(n - 1) % 2], (n - 1) // 2, (n - 1) % 2)

    @pl.when(step == 4)
    def _():
        lane = lax.broadcasted_iota(jnp.int32, (ROWS, 128), 1)
        stats[...] = jnp.zeros_like(stats)
        for j in range(4):
            wide = jnp.zeros((ROWS, 128), F32)
            for s in range(4):
                at_lane = (at[1] ^ j) % 2 * 4 + s
                wide = jnp.where(lane == at_lane, jnp.sum(sums[s, j], axis=1, keepdims=True), wide)
            wide = jnp.concatenate([wide, jnp.zeros((256 - ROWS, 128), F32)], axis=0)
            stats[(at[1] ^ j) // 2] += wide.T[:8]


def logits_call(at, own, nbr, far, head, mate, got, tgt):
    def once(*shape):
        return pl.BlockSpec(
            shape, lambda s, at: (0,) * len(shape), pipeline_mode=pl.Buffered(1)
        )

    def part(s):
        return jnp.minimum(s // 2, 1)

    def tile(s, at):
        done = jnp.maximum(s - 1, 0)
        return (0, 0, done % 2 * 2 + done // 2)

    return pl.pallas_call(
        logits_kernel,
        grid_spec=pltpu.PrefetchScalarGridSpec(
            num_scalar_prefetch=1,
            grid=(5,),
            in_specs=[once(ROWS, 2 * HALF_D)] * 2
            + [once(8, 4, 48, 896)]
            + [
                pl.BlockSpec((HALF_D, TILE), lambda s, at: (0, at[1] * 2 + part(s))),
                pl.BlockSpec((HALF_D, TILE), lambda s, at: (0, part(s))),
            ]
            + [pl.BlockSpec((c, TILE), lambda s, at: (0, part(s))) for c in CHUNKS] * 2
            + [whole(2, ROWS, 128)],
            out_specs=[pl.BlockSpec((4, ROWS, TILE), tile), whole(2, 8, 256)],
            scratch_shapes=[
                pltpu.VMEM((4 * ROWS, 2 * HALF_D), BF16),
                pltpu.VMEM((4 * ROWS, TILE), F32),
                pltpu.VMEM((4 * ROWS, TILE), F32),
                pltpu.VMEM((4, 4, ROWS, 128), F32),
            ],
        ),
        out_shape=[
            jax.ShapeDtypeStruct((4, ROWS, 4 * TILE), F32),
            jax.ShapeDtypeStruct((2, 8, 256), F32),
        ],
        compiler_params=pltpu.CompilerParams(vmem_limit_bytes=VMEM),
        cost_estimate=pl.CostEstimate(
            flops=4 * ROWS * 4 * TILE * 2 * HALF_D * 2, bytes_accessed=16 << 20, transcendentals=1 << 21
        ),
        name="logits",
    )(at, own, nbr, far, head, mate, *got, tgt)


def grad_kernel(at, logits, stats, tgt, mask, out, scales, *, i):
    step = pl.program_id(0)

    @pl.when(step == 0)
    def _():
        for j in (i, 2 + i):
            block = at[1] ^ j
            total = stats[block // 2].T[:ROWS]
            total = jnp.where(block % 2 == 0, total[:, 0:2], total[:, 4:6])
            weight = loss_scale * mask[j // 2]
            scales[0, j] = (1.0 + kl_weight) * weight / total[:, 0:1]
            scales[1, j] = kl_weight * weight / total[:, 1:2]

    core, part = step // 2, step % 2
    column = lax.broadcasted_iota(jnp.int32, (48, TILE), 1)
    column = column + (jnp.where(core == 0, at[4], at[5]) + part * TILE)

    for pair in range(2):
        for g in range(4):
            here = slice(g * 48, g * 48 + 48)
            both = [logits[pair * 2, here], logits[pair * 2 + 1, here]]
            target, weight = tgt[pair, here], loss_scale * mask[pair, here]
            target = jnp.concatenate([target, target], axis=1)
            weight = jnp.concatenate([weight, weight], axis=1)
            hit = jnp.where(column == target, weight, 0.0)
            own = both[i]
            shared = both[1 - i].astype(BF16).astype(F32)
            own_scale, partner_scale = (
                jnp.concatenate([scales[n, pair * 2 + i, here]] * 2, axis=1) for n in range(2)
            )
            slope = own * (1.0 / softcap_limit)
            value = jnp.exp(own) * own_scale - hit - jnp.exp(shared) * partner_scale
            out[pair, here] = (value * (1.0 - slope * slope)).astype(BF16)


def grad_call(at, logits, stats, tgt, mask, i):
    out = pl.BlockSpec((2, ROWS, TILE), lambda s, at: (0, 0, s))
    return pl.pallas_call(
        functools.partial(grad_kernel, i=i),
        grid_spec=pltpu.PrefetchScalarGridSpec(
            num_scalar_prefetch=1,
            grid=(4,),
            in_specs=[
                pl.BlockSpec((4, ROWS, TILE), lambda s, at: (0, 0, s)),
                whole(2, 8, 256),
                whole(2, ROWS, 128),
                whole(2, ROWS, 128),
            ],
            out_specs=out,
            scratch_shapes=[pltpu.VMEM((2, 4, ROWS, 128), F32)],
        ),
        out_shape=jax.ShapeDtypeStruct((2, ROWS, 4 * TILE), BF16),
        compiler_params=pltpu.CompilerParams(vmem_limit_bytes=VMEM),
        name="logit_grad",
    )(at, logits, stats, tgt, mask)


def terms_kernel(at, *refs, ks, add, last):
    refs = list(refs)
    left, right = [], []
    for k in ks:
        grad, head, mate = refs[:3]
        refs = refs[3:]
        order = (0, 1) if k < 2 else (1, 0)
        left.append(jnp.concatenate([grad[t] for t in order], axis=0))
        right += [head[...], mate[...]]
    total = jnp.dot(
        jnp.concatenate(left, axis=1),
        jnp.concatenate(right, axis=0),
        preferred_element_type=F32,
    )
    if add:
        total = total + refs.pop(0)[...]
    if not last:
        refs[0][...] = total
        return
    outs, scratch = refs[:4], refs[4]
    for tok in range(2):
        for y in range(4):
            begin = tok * ROWS + y * 48
            scratch[y, tok] = total[begin : begin + 48]
    for k in range(4):
        outs[k][...] = scratch[at[2] ^ k].astype(outs[k].dtype)


def terms_call(at, grads, head, mate, ks, acc=None, last=False):
    tile = pl.BlockSpec((2 * ROWS, WIDE), lambda s, at: (0, s))
    in_specs, args = [], []
    for k, grad in zip(ks, grads):
        weights = pl.BlockSpec((QUARTER, WIDE), lambda s, at, k=k: (at[1] ^ k, s))
        in_specs += [pl.BlockSpec((2, ROWS, 4 * TILE), lambda s, at: (0, 0, 0)), weights, weights]
        args += [grad, head, mate]
    out_specs, scratch = tile, []
    out_shape = jax.ShapeDtypeStruct((2 * ROWS, HALF_D), F32)
    if acc is not None:
        in_specs.append(tile)
        args.append(acc)
    if last:
        out_specs = [pl.BlockSpec((2, 48, WIDE), lambda s, at: (0, 0, s))] * 4
        out_shape = [jax.ShapeDtypeStruct((2, 48, HALF_D), t) for t in (F32, BF16, BF16, BF16)]
        scratch = [pltpu.VMEM((4, 2, 48, WIDE), F32)]
    return pl.pallas_call(
        functools.partial(terms_kernel, ks=ks, add=acc is not None, last=last),
        grid_spec=pltpu.PrefetchScalarGridSpec(
            num_scalar_prefetch=1,
            grid=(HALF_D // WIDE,),
            in_specs=in_specs,
            out_specs=out_specs,
            scratch_shapes=scratch,
        ),
        out_shape=out_shape,
        compiler_params=pltpu.CompilerParams(vmem_limit_bytes=VMEM * 3 // 5),
        cost_estimate=pl.CostEstimate(
            flops=2 * 2 * ROWS * HALF_D * 2 * QUARTER * len(ks),
            bytes_accessed=(6 << 20) * len(ks),
            transcendentals=0,
        ),
        name="gradient_terms",
    )(at, *args)


def rows_kernel(at, *refs):
    parts, out_ref = refs[:4], refs[4]
    total = parts[0][...]
    for part in parts[1:]:
        total = total + part[...].astype(F32)
    out = lax.broadcasted_iota(jnp.int32, (128, 96), 0)
    src = lax.broadcasted_iota(jnp.int32, (128, 96), 1)
    i = out & 7
    wanted = ((out >> 6) ^ at[0]) * 48 + ((out >> 3) & 7) * 6 + i
    pick = jnp.where((src == wanted) & (i < 6), 1.0, 0.0).astype(BF16)
    low = jnp.dot(pick, total.reshape(96, 896).astype(BF16), preferred_element_type=F32)
    out_ref[...] = low.reshape(16, 8, 896).astype(BF16)


def rows_call(at, parts):
    return pl.pallas_call(
        rows_kernel,
        grid_spec=pltpu.PrefetchScalarGridSpec(
            num_scalar_prefetch=1,
            grid=(2,),
            in_specs=[pl.BlockSpec((2, 48, 896), lambda s, at: (0, 0, s))] * 4,
            out_specs=pl.BlockSpec((16, 8, 896), lambda s, at: (0, 0, s)),
        ),
        out_shape=jax.ShapeDtypeStruct((16, 8, HALF_D), BF16),
        compiler_params=pltpu.CompilerParams(vmem_limit_bytes=VMEM // 3),
        name="rows",
    )(at, *parts)


def add_over_slice(stats):
    for axis in ((*LINE, "y"), "z"):
        spread = jnp.broadcast_to(stats[None], (lax.axis_size(axis), *stats.shape))
        stats = jnp.sum(lax.all_to_all(spread, axis, 0, 0, tiled=True), axis=0)
    return stats


def pick_rows(block, count, core):
    out = lax.broadcasted_iota(jnp.int32, (count, 2 * count), 0)
    src = lax.broadcasted_iota(jnp.int32, (count, 2 * count), 1)
    pick = (src == out // 6 * 12 + core * 6 + out % 6).astype(BF16)
    return jnp.dot(pick, block, preferred_element_type=F32).astype(BF16)


def shards(hidden, head, targets, loss_mask):
    rep, tok, y, z, core = (lax.axis_index(a) for a in ("rep", "tok", "y", "z", "core"))
    x = tok * 2 + rep
    states = hidden[0]

    sync = lax.optimization_barrier

    scal = jnp.stack([targets, loss_mask]).reshape(2, 32, 2, 6)
    scal = lax.dynamic_index_in_dim(scal, core, 2, keepdims=False).reshape(2, ROWS)
    slab = pick_rows(lax.dynamic_slice(states, (z * 48, y * 896), (48, 896)), 24, core)
    piece = jnp.concatenate([line_xor(slab, 2), line_xor(slab, 3)], axis=0)[None]
    far_scal = line_xor(scal, 2)
    sent = [
        lax.dynamic_slice(head, (sum(CHUNKS[:n]), (3 - x) * QUARTER), (CHUNKS[n], QUARTER))
        for n in range(3)
    ]
    piece, far_scal, *sent = sync((piece, far_scal, *sent))
    got = [line_xor(sent[0], 3)]
    piece = jnp.concatenate([piece] + [axis_xor(piece, "y", k) for k in (1, 2, 3)])
    own = pick_rows(states, ROWS, core)
    piece, own, got[0], sent[1] = sync((piece, own, got[0], sent[1]))
    got.append(line_xor(sent[1], 3))
    far = lax.all_gather(piece[None], "z", axis=0, tiled=True)
    nbr = line_xor(own, 1)

    voc = (y * 8 + z) * 2
    begin = [(voc + c) * 2048 + x * QUARTER for c in (core, 1 - core)]
    at = jnp.stack([tok, x, y, z, begin[0], begin[1]]).astype(jnp.int32)
    scal = jnp.stack([scal, far_scal], axis=1)
    mask = scal[1].astype(F32)
    tgt_wide = jnp.broadcast_to(scal[0][..., None], (2, ROWS, 128))
    mask_wide = jnp.broadcast_to(mask[..., None], (2, ROWS, 128))

    head_t = head.T
    head_t, cut = sync((head_t, head))
    cut = lax.dynamic_slice(cut, (0, x * QUARTER), (HALF_D, QUARTER))
    head_t, tgt_wide, mask_wide, got[1], nbr, sent[2], cut = sync(
        (head_t, tgt_wide, mask_wide, got[1], nbr, sent[2], cut)
    )
    got.append(line_xor(sent[2], 3))
    mate = axis_xor(cut, "core", 1)
    got_mate = [axis_xor(g, "core", 1) for g in got]
    got = got + got_mate

    logits, stats = logits_call(at, own, nbr, far, head, mate, got, tgt_wide)
    head_t, stats = sync((head_t, stats))
    mate_t = axis_xor(head_t, "core", 1)
    stats = add_over_slice(stats)

    theirs = grad_call(at, logits, stats, tgt_wide, mask_wide, 1)
    near, cross_part = line_xor(theirs, 1), line_xor(theirs, 3)
    mine = grad_call(at, logits, stats, tgt_wide, mask_wide, 0)
    grads = [mine, near, line_xor(mine, 2), cross_part]
    terms = terms_call(at, grads[:1], head_t, mate_t, (0,))
    terms = terms_call(at, grads[3:], head_t, mate_t, (3,), terms)
    parts = list(terms_call(at, grads[1:3], head_t, mate_t, (1, 2), terms, last=True))

    stats, parts[0] = sync((stats, parts[0]))
    stats = lax.dynamic_index_in_dim(stats.reshape(4, 4, 256), x, 0, keepdims=False)
    own_total, partner_total, picked, cross = (stats[s, :ROWS] for s in range(4))
    own_lse, partner_lse = jnp.log(own_total), jnp.log(partner_total)
    loss = mask[0] * (
        own_lse - picked + kl_weight * (cross / partner_total - partner_lse + own_lse)
    )
    pair = jnp.stack([loss, axis_xor(loss, "core", 1)]).reshape(2, 32, 6)
    pair = jnp.where(core == 0, pair, pair[::-1])
    token_loss = pair.transpose(1, 0, 2).reshape(1, 384)

    parts = [parts[0]] + [axis_xor(parts[k], "y", k) for k in (1, 2, 3)]
    token_loss, parts[0] = sync((token_loss, parts[0]))
    low = lax.all_to_all(rows_call(at, parts), ("tok", "z"), 0, 0, tiled=True)
    total = jnp.sum(low.reshape(2, 8, 8, HALF_D).astype(F32), axis=1)[:, :6]
    out = jnp.concatenate([total[0], total[1]], axis=1)
    return out.astype(BF16)[None], token_loss


def solution(mesh):
    fine = Mesh(
        mesh.devices.reshape(2, 2, N_Y, N_Z, N_C), ("rep", "tok", "y", "z", "core")
    )
    voc = ("y", "z", "core")
    placed = (P("rep", "tok", None), P("tok", voc), P("tok"), P("tok"))
    return jax.shard_map(
        shards,
        mesh=fine,
        in_specs=placed,
        out_specs=(P("rep", ("tok", *voc), None), P("rep", "tok")),
        check_vma=False,
    )
```

```python
import functools

import jax
import jax.numpy as jnp
from jax import lax
from jax.experimental import pallas as pl
from jax.experimental.pallas import tpu as pltpu
from jax.sharding import Mesh, PartitionSpec as P

softcap_limit = 30.0
kl_weight = 0.5
loss_scale = 16.0

N_Y, N_Z, N_C, N_X = 4, 8, 2, 4
LINE = ("rep", "tok")
ROWS = 192
QUARTER = 512
HALF_D = 1792
CHUNKS = (1536, 256)
TILE = 256
WIDE = 896
VMEM = 50 * 1024 * 1024
F32, BF16 = jnp.float32, jnp.bfloat16


def line_xor(block, k):
    k = (k % 2) * 2 + k // 2
    return lax.ppermute(block, LINE, [(x, x ^ k) for x in range(N_X)])


def axis_xor(block, axis, k):
    return lax.ppermute(block, axis, [(i, i ^ k) for i in range(lax.axis_size(axis))])


def whole(*shape):
    return pl.BlockSpec(shape, lambda s, at: (0,) * len(shape))


def logits_kernel(at, own, nbr, *refs):
    far, head, mate, got, tgt = refs[0], refs[1], refs[2], refs[3:7], refs[7]
    logits, stats, rows, raws, sums = refs[8], refs[9], refs[10], refs[11:13], refs[13]
    step = pl.program_id(0)
    tok, y = at[0], at[2]

    @pl.when(step == 0)
    def _():
        for side in range(2):
            half = tok if side == 0 else 1 - tok
            begin = pl.multiple_of(half * HALF_D, 128)
            to = pl.ds(side * HALF_D, HALF_D)
            rows[0:ROWS, to] = own[:, pl.ds(begin, HALF_D)]
            rows[ROWS : 2 * ROWS, to] = nbr[:, pl.ds(begin, HALF_D)]
        for k in range(4):
            d = y ^ k
            column = pl.multiple_of((d // 2 ^ tok) * HALF_D + d % 2 * 896, 128)
            rows[2 * ROWS :, pl.ds(column, 896)] = far[:, k].reshape(2 * ROWS, 896)
        sums[...] = jnp.zeros_like(sums)

    lane = lax.broadcasted_iota(jnp.int32, (48, TILE), 1)

    def product(raw, head, got):
        weights = jnp.concatenate([head[...]] + [chunk[...] for chunk in got], axis=0)
        raw[...] = jnp.dot(rows[...], weights, preferred_element_type=F32)

    def work(raw, part, core):
        column = lane + (at[4 + core] + part * TILE)
        for chunk in range(8):
            pair, g = chunk // 4, chunk % 4
            here = slice(g * 48, g * 48 + 48)
            if pair == 0:
                both = [raw[here], raw[ROWS + g * 48 : ROWS + g * 48 + 48]]
            else:
                begin = 2 * ROWS + g * 96
                pieces = [raw[begin + 24 * i : begin + 24 * i + 24] for i in range(4)]
                both = [jnp.concatenate(pieces[i::2], axis=0) for i in range(2)]
            both = [softcap_limit * jnp.tanh(v * (1.0 / softcap_limit)) for v in both]
            target = tgt[pair, here]
            hit = column == jnp.concatenate([target, target], axis=1)
            shared = [v.astype(BF16).astype(F32) for v in both]
            partner = [jnp.exp(v) for v in shared]
            for i in range(2):
                j = pair * 2 + i
                mine = both[i]
                logits[j, here] = mine
                terms = (
                    jnp.exp(mine),
                    partner[1 - i],
                    jnp.where(hit, mine, 0.0),
                    partner[1 - i] * (shared[1 - i] - mine),
                )
                for s, term in enumerate(terms):
                    sums[s, j, here] += term[:, :128] + term[:, 128:]

    for n in range(5):
        @pl.when(step == n)
        def _(n=n):
            if n < 4:
                core = n % 2
                product(raws[n % 2], (head, mate)[core], got[core * 2 : core * 2 + 2])
            if n > 0:
                work(raws[(n - 1) % 2], (n - 1) // 2, (n - 1) % 2)

    @pl.when(step == 4)
    def _():
        lane = lax.broadcasted_iota(jnp.int32, (ROWS, 128), 1)
        stats[...] = jnp.zeros_like(stats)
        for j in range(4):
            wide = jnp.zeros((ROWS, 128), F32)
            for s in range(4):
                at_lane = (at[1] ^ j) % 2 * 4 + s
                wide = jnp.where(lane == at_lane, jnp.sum(sums[s, j], axis=1, keepdims=True), wide)
            wide = jnp.concatenate([wide, jnp.zeros((256 - ROWS, 128), F32)], axis=0)
            stats[(at[1] ^ j) // 2] += wide.T[:8]


def logits_call(at, own, nbr, far, head, mate, got, tgt):
    def once(*shape):
        return pl.BlockSpec(
            shape, lambda s, at: (0,) * len(shape), pipeline_mode=pl.Buffered(1)
        )

    def part(s):
        return jnp.minimum(s // 2, 1)

    def tile(s, at):
        done = jnp.maximum(s - 1, 0)
        return (0, 0, done % 2 * 2 + done // 2)

    return pl.pallas_call(
        logits_kernel,
        grid_spec=pltpu.PrefetchScalarGridSpec(
            num_scalar_prefetch=1,
            grid=(5,),
            in_specs=[once(ROWS, 2 * HALF_D)] * 2
            + [once(8, 4, 48, 896)]
            + [
                pl.BlockSpec((HALF_D, TILE), lambda s, at: (0, at[1] * 2 + part(s))),
                pl.BlockSpec((HALF_D, TILE), lambda s, at: (0, part(s))),
            ]
            + [pl.BlockSpec((c, TILE), lambda s, at: (0, part(s))) for c in CHUNKS] * 2
            + [whole(2, ROWS, 128)],
            out_specs=[pl.BlockSpec((4, ROWS, TILE), tile), whole(2, 8, 256)],
            scratch_shapes=[
                pltpu.VMEM((4 * ROWS, 2 * HALF_D), BF16),
                pltpu.VMEM((4 * ROWS, TILE), F32),
                pltpu.VMEM((4 * ROWS, TILE), F32),
                pltpu.VMEM((4, 4, ROWS, 128), F32),
            ],
        ),
        out_shape=[
            jax.ShapeDtypeStruct((4, ROWS, 4 * TILE), F32),
            jax.ShapeDtypeStruct((2, 8, 256), F32),
        ],
        compiler_params=pltpu.CompilerParams(vmem_limit_bytes=VMEM),
        cost_estimate=pl.CostEstimate(
            flops=4 * ROWS * 4 * TILE * 2 * HALF_D * 2, bytes_accessed=16 << 20, transcendentals=1 << 21
        ),
        name="logits",
    )(at, own, nbr, far, head, mate, *got, tgt)


def grad_kernel(at, logits, stats, tgt, mask, mine, theirs, scales):
    step = pl.program_id(0)

    @pl.when(step == 0)
    def _():
        for j in range(4):
            block = at[1] ^ j
            total = stats[block // 2].T[:ROWS]
            total = jnp.where(block % 2 == 0, total[:, 0:2], total[:, 4:6])
            weight = loss_scale * mask[j // 2]
            scales[0, j] = (1.0 + kl_weight) * weight / total[:, 0:1]
            scales[1, j] = kl_weight * weight / total[:, 1:2]

    core, part = step // 2, step % 2
    column = lax.broadcasted_iota(jnp.int32, (48, TILE), 1)
    column = column + (jnp.where(core == 0, at[4], at[5]) + part * TILE)

    for pair in range(2):
        for g in range(4):
            here = slice(g * 48, g * 48 + 48)
            both = [logits[pair * 2, here], logits[pair * 2 + 1, here]]
            target, weight = tgt[pair, here], loss_scale * mask[pair, here]
            target = jnp.concatenate([target, target], axis=1)
            weight = jnp.concatenate([weight, weight], axis=1)
            hit = jnp.where(column == target, weight, 0.0)
            for i in range(2):
                own = both[i]
                shared = both[1 - i].astype(BF16).astype(F32)
                own_scale, partner_scale = (
                    jnp.concatenate([scales[n, pair * 2 + i, here]] * 2, axis=1) for n in range(2)
                )
                slope = own * (1.0 / softcap_limit)
                value = jnp.exp(own) * own_scale - hit - jnp.exp(shared) * partner_scale
                (mine, theirs)[i][pair, here] = (value * (1.0 - slope * slope)).astype(BF16)


def grad_call(at, logits, stats, tgt, mask):
    out = pl.BlockSpec((2, ROWS, TILE), lambda s, at: (0, 0, s))
    return pl.pallas_call(
        grad_kernel,
        grid_spec=pltpu.PrefetchScalarGridSpec(
            num_scalar_prefetch=1,
            grid=(4,),
            in_specs=[
                pl.BlockSpec((4, ROWS, TILE), lambda s, at: (0, 0, s)),
                whole(2, 8, 256),
                whole(2, ROWS, 128),
                whole(2, ROWS, 128),
            ],
            out_specs=[out, out],
            scratch_shapes=[pltpu.VMEM((2, 4, ROWS, 128), F32)],
        ),
        out_shape=[jax.ShapeDtypeStruct((2, ROWS, 4 * TILE), BF16)] * 2,
        compiler_params=pltpu.CompilerParams(vmem_limit_bytes=VMEM),
        name="logit_grad",
    )(at, logits, stats, tgt, mask)


def terms_kernel(at, *refs, ks, add, last):
    refs = list(refs)
    left, right = [], []
    for k in ks:
        grad, head, mate = refs[:3]
        refs = refs[3:]
        order = (0, 1) if k < 2 else (1, 0)
        left.append(jnp.concatenate([grad[t] for t in order], axis=0))
        right += [head[...], mate[...]]
    total = jnp.dot(
        jnp.concatenate(left, axis=1),
        jnp.concatenate(right, axis=0),
        preferred_element_type=F32,
    )
    if add:
        total = total + refs.pop(0)[...]
    if not last:
        refs[0][...] = total
        return
    outs, scratch = refs[:4], refs[4]
    for tok in range(2):
        for y in range(4):
            begin = tok * ROWS + y * 48
            scratch[y, tok] = total[begin : begin + 48]
    for k in range(4):
        outs[k][...] = scratch[at[2] ^ k].astype(outs[k].dtype)


def terms_call(at, grads, head, mate, ks, acc=None, last=False):
    tile = pl.BlockSpec((2 * ROWS, WIDE), lambda s, at: (0, s))
    in_specs, args = [], []
    for k, grad in zip(ks, grads):
        weights = pl.BlockSpec((QUARTER, WIDE), lambda s, at, k=k: (at[1] ^ k, s))
        in_specs += [pl.BlockSpec((2, ROWS, 4 * TILE), lambda s, at: (0, 0, 0)), weights, weights]
        args += [grad, head, mate]
    out_specs, scratch = tile, []
    out_shape = jax.ShapeDtypeStruct((2 * ROWS, HALF_D), F32)
    if acc is not None:
        in_specs.append(tile)
        args.append(acc)
    if last:
        out_specs = [pl.BlockSpec((2, 48, WIDE), lambda s, at: (0, 0, s))] * 4
        out_shape = [jax.ShapeDtypeStruct((2, 48, HALF_D), t) for t in (F32, BF16, BF16, BF16)]
        scratch = [pltpu.VMEM((4, 2, 48, WIDE), F32)]
    return pl.pallas_call(
        functools.partial(terms_kernel, ks=ks, add=acc is not None, last=last),
        grid_spec=pltpu.PrefetchScalarGridSpec(
            num_scalar_prefetch=1,
            grid=(HALF_D // WIDE,),
            in_specs=in_specs,
            out_specs=out_specs,
            scratch_shapes=scratch,
        ),
        out_shape=out_shape,
        compiler_params=pltpu.CompilerParams(vmem_limit_bytes=VMEM * 3 // 5),
        cost_estimate=pl.CostEstimate(
            flops=2 * 2 * ROWS * HALF_D * 2 * QUARTER * len(ks),
            bytes_accessed=(6 << 20) * len(ks),
            transcendentals=0,
        ),
        name="gradient_terms",
    )(at, *args)


def rows_kernel(at, *refs):
    parts, out_ref = refs[:4], refs[4]
    total = parts[0][...]
    for part in parts[1:]:
        total = total + part[...].astype(F32)
    out = lax.broadcasted_iota(jnp.int32, (128, 96), 0)
    src = lax.broadcasted_iota(jnp.int32, (128, 96), 1)
    i = out & 7
    wanted = ((out >> 6) ^ at[0]) * 48 + ((out >> 3) & 7) * 6 + i
    pick = jnp.where((src == wanted) & (i < 6), 1.0, 0.0).astype(BF16)
    low = jnp.dot(pick, total.reshape(96, 896).astype(BF16), preferred_element_type=F32)
    out_ref[...] = low.reshape(16, 8, 896).astype(BF16)


def rows_call(at, parts):
    return pl.pallas_call(
        rows_kernel,
        grid_spec=pltpu.PrefetchScalarGridSpec(
            num_scalar_prefetch=1,
            grid=(2,),
            in_specs=[pl.BlockSpec((2, 48, 896), lambda s, at: (0, 0, s))] * 4,
            out_specs=pl.BlockSpec((16, 8, 896), lambda s, at: (0, 0, s)),
        ),
        out_shape=jax.ShapeDtypeStruct((16, 8, HALF_D), BF16),
        compiler_params=pltpu.CompilerParams(vmem_limit_bytes=VMEM // 3),
        name="rows",
    )(at, *parts)


def add_over_slice(stats):
    for axis in ((*LINE, "y"), "z"):
        spread = jnp.broadcast_to(stats[None], (lax.axis_size(axis), *stats.shape))
        stats = jnp.sum(lax.all_to_all(spread, axis, 0, 0, tiled=True), axis=0)
    return stats


def pick_rows(block, count, core):
    out = lax.broadcasted_iota(jnp.int32, (count, 2 * count), 0)
    src = lax.broadcasted_iota(jnp.int32, (count, 2 * count), 1)
    pick = (src == out // 6 * 12 + core * 6 + out % 6).astype(BF16)
    return jnp.dot(pick, block, preferred_element_type=F32).astype(BF16)


def shards(hidden, head, targets, loss_mask):
    rep, tok, y, z, core = (lax.axis_index(a) for a in ("rep", "tok", "y", "z", "core"))
    x = tok * 2 + rep
    states = hidden[0]

    sync = lax.optimization_barrier

    scal = jnp.stack([targets, loss_mask]).reshape(2, 32, 2, 6)
    scal = lax.dynamic_index_in_dim(scal, core, 2, keepdims=False).reshape(2, ROWS)
    slab = pick_rows(lax.dynamic_slice(states, (z * 48, y * 896), (48, 896)), 24, core)
    piece = jnp.concatenate([line_xor(slab, 2), line_xor(slab, 3)], axis=0)[None]
    far_scal = line_xor(scal, 2)
    sent = [
        lax.dynamic_slice(head, (n * CHUNKS[0], (3 - x) * QUARTER), (CHUNKS[n], QUARTER))
        for n in range(2)
    ]
    piece, far_scal, *sent = sync((piece, far_scal, *sent))
    got = [line_xor(sent[0], 3)]
    piece = jnp.concatenate([piece] + [axis_xor(piece, "y", k) for k in (1, 2, 3)])
    own = pick_rows(states, ROWS, core)
    piece, own = sync((piece, own))
    far = lax.all_gather(piece[None], "z", axis=0, tiled=True)
    nbr = line_xor(own, 1)

    voc = (y * 8 + z) * 2
    begin = [(voc + c) * 2048 + x * QUARTER for c in (core, 1 - core)]
    at = jnp.stack([tok, x, y, z, begin[0], begin[1]]).astype(jnp.int32)
    scal = jnp.stack([scal, far_scal], axis=1)
    mask = scal[1].astype(F32)
    tgt_wide = jnp.broadcast_to(scal[0][..., None], (2, ROWS, 128))
    mask_wide = jnp.broadcast_to(mask[..., None], (2, ROWS, 128))

    head_t = head.T
    head_t, cut = sync((head_t, head))
    cut = lax.dynamic_slice(cut, (0, x * QUARTER), (HALF_D, QUARTER))
    head_t, tgt_wide, mask_wide, got[0], nbr, sent[1], cut = sync(
        (head_t, tgt_wide, mask_wide, got[0], nbr, sent[1], cut)
    )
    got.append(line_xor(sent[1], 3))
    mate = axis_xor(cut, "core", 1)
    got_mate = [axis_xor(g, "core", 1) for g in got]
    got = got + got_mate

    logits, stats = logits_call(at, own, nbr, far, head, mate, got, tgt_wide)
    head_t, stats = sync((head_t, stats))
    mate_t = axis_xor(head_t, "core", 1)
    stats = add_over_slice(stats)

    mine, theirs = grad_call(at, logits, stats, tgt_wide, mask_wide)
    grads = [mine, line_xor(theirs, 1), line_xor(mine, 2), line_xor(theirs, 3)]
    terms = terms_call(at, grads[:1], head_t, mate_t, (0,))
    terms = terms_call(at, grads[1:2], head_t, mate_t, (1,), terms)
    parts = list(terms_call(at, grads[2:], head_t, mate_t, (2, 3), terms, last=True))

    stats, parts[0] = sync((stats, parts[0]))
    stats = lax.dynamic_index_in_dim(stats.reshape(4, 4, 256), x, 0, keepdims=False)
    own_total, partner_total, picked, cross = (stats[s, :ROWS] for s in range(4))
    own_lse, partner_lse = jnp.log(own_total), jnp.log(partner_total)
    loss = mask[0] * (
        own_lse - picked + kl_weight * (cross / partner_total - partner_lse + own_lse)
    )
    pair = jnp.stack([loss, axis_xor(loss, "core", 1)]).reshape(2, 32, 6)
    pair = jnp.where(core == 0, pair, pair[::-1])
    token_loss = pair.transpose(1, 0, 2).reshape(1, 384)

    parts = [parts[0]] + [axis_xor(parts[k], "y", k) for k in (1, 2, 3)]
    token_loss, parts[0] = sync((token_loss, parts[0]))
    low = lax.all_to_all(rows_call(at, parts), ("tok", "z"), 0, 0, tiled=True)
    total = jnp.sum(low.reshape(2, 8, 8, HALF_D).astype(F32), axis=1)[:, :6]
    out = jnp.concatenate([total[0], total[1]], axis=1)
    return out.astype(BF16)[None], token_loss


def solution(mesh):
    fine = Mesh(
        mesh.devices.reshape(2, 2, N_Y, N_Z, N_C), ("rep", "tok", "y", "z", "core")
    )
    voc = ("y", "z", "core")
    placed = (P("rep", "tok", None), P("tok", voc), P("tok"), P("tok"))
    return jax.shard_map(
        shards,
        mesh=fine,
        in_specs=placed,
        out_specs=(P("rep", ("tok", *voc), None), P("rep", "tok")),
        check_vma=False,
    )
```
